256 devices in a mesh: gy: 8 (over y_hi, x), gx: 32 (over y_lo, z, core).
Axes of the slice: x: 4, y: 4 (y_hi: 2, y_lo: 2; y = y_hi * 2 + y_lo), z: 8, core: 2. Of those that a mesh axis runs over, the one named last changes fastest.
Arguments:
- queries: bfloat16 [128, 512, 512], P('gy', 'gx'), may hold values from -7 to 7
- key_vectors: bfloat16 [128, 512, 512], P('gy', 'gx'), may hold values from -7 to 7
- values: bfloat16 [128, 512, 512], P('gy', 'gx'), may hold values from -6 to 6
- residual: bfloat16 [128, 512, 512], P('gy', 'gx'), may hold values from -60 to 60
- cotangent: bfloat16 [128, 512, 512], P('gy', 'gx'), may hold values from -6 to 6
- out_proj: bfloat16 [512, 512], replicated, may hold values from -0.25 to 0.25
- norm_gain: float32 [512], replicated, may hold values from 0.5 to 1.5
- router: bfloat16 [512, 64], replicated, may hold values from -0.25 to 0.25
- expert_in: bfloat16 [64, 512, 2048], P('gx'), may hold values from -0.25 to 0.25
- expert_out: bfloat16 [64, 2048, 512], P('gx'), may hold values from -0.125 to 0.125
- expert_id: int32 [128, 512], P('gy', 'gx'), may hold values from 0 to 63, as said below
- slot_index: int32 [128, 512], P('gy', 'gx'), may hold values from 0 to 7
Outputs:
- grad_queries: bfloat16 [128, 512, 512], P('gy', 'gx')
- grad_keys: bfloat16 [128, 512, 512], P('gy', 'gx')
- grad_values: bfloat16 [128, 512, 512], P('gy', 'gx')
- grad_input: bfloat16 [128, 512, 512], P('gy', 'gx')
- grad_out_proj: bfloat16 [512, 512], replicated
- grad_gain: float32 [512], replicated
- grad_router: float32 [512, 64], replicated
- grad_expert_in: bfloat16 [64, 512, 2048], P('gx', None, 'gy')
- grad_expert_out: bfloat16 [64, 2048, 512], P('gx', 'gy')
The draws below stay inside these ranges and needn't reach their ends.
Inputs may be any that keep to these rules, and one draw needn't show every extreme that they name: `expert_id`: within each aligned 16 x 16 tile no two tokens share both expert and slot, so an expert has at most 8 tokens of a tile; in every row of tiles one expert fills all 8 of its slots in every tile of that row.
All inputs are finite; a program needn't handle non-finite values.
Results may differ from the reference program's by a relative error of at most 0.015.
Values may be sent and summed in bfloat16 or wider, within the bound.
No kernel may reach another device: no remote copies, remote signals or barrier semaphores. Data moves between devices by JAX's collectives and lax.ppermute only.
A program may use at most 128 MiB of HBM per device.

```python
import jax
import jax.numpy as jnp
from jax import lax

D = 512
HEADS = 16
HID = 2048
WIN = 16
SHIFT = 8
HEAD_DIM = 32
IMG_ROWS = 128
IMG_COLS = 512
EXPERTS = 64
CAP = 8
N_GY = 8
N_GX = 32


def draw_queries(key, part):
    key = jax.random.fold_in(key, 1)
    shape = (IMG_ROWS, IMG_COLS, D)
    base = jnp.clip(jax.random.normal(key, shape, jnp.float32), -6.0, 6.0)
    return base.astype(jnp.bfloat16)


def draw_key_vectors(key, part):
    key = jax.random.fold_in(key, 2)
    shape = (IMG_ROWS, IMG_COLS, D)
    base = jnp.clip(jax.random.normal(key, shape, jnp.float32), -6.0, 6.0)
    return base.astype(jnp.bfloat16)


def draw_residual(key, part):
    key = jax.random.fold_in(key, 3)
    row_key, col_key, base_key = jax.random.split(key, 3)
    shape = (IMG_ROWS, IMG_COLS, D)
    row_scale = jnp.exp(jax.random.uniform(row_key, (IMG_ROWS, IMG_COLS, 1), jnp.float32, -1.204, 1.0986))
    col_scale = jnp.exp(jax.random.uniform(col_key, (1, 1, D), jnp.float32, -1.204, 1.0986))
    base = jnp.clip(jax.random.normal(base_key, shape, jnp.float32), -6.0, 6.0)
    return (base * row_scale * col_scale).astype(jnp.bfloat16)


def routing_table(key):
    key = jax.random.fold_in(key, 500)
    pick_key, order_key, place_key = jax.random.split(key, 3)
    tiles_down = IMG_ROWS // WIN
    tiles_across = IMG_COLS // WIN
    tile_count = tiles_down * tiles_across
    slot_count = EXPERTS * CAP
    tokens = WIN * WIN
    forced = jax.random.randint(pick_key, (tiles_down, 1), 0, EXPERTS)
    forced = jnp.broadcast_to(forced, (tiles_down, tiles_across)).reshape(tile_count, 1)
    ranks = jax.vmap(lambda subkey: jax.random.permutation(subkey, slot_count))(jax.random.split(order_key, tile_count))
    owner = jnp.arange(slot_count)[None, :] // CAP
    scores = jnp.where(owner == forced, ranks - slot_count, ranks)
    chosen = jnp.argsort(scores, axis=1, stable=True)[:, :tokens]
    spread = jax.vmap(lambda subkey: jax.random.permutation(subkey, tokens))(jax.random.split(place_key, tile_count))
    chosen = jnp.take_along_axis(chosen, spread, axis=1)
    layout = chosen.reshape(tiles_down, tiles_across, WIN, WIN).transpose(0, 2, 1, 3).reshape(IMG_ROWS, IMG_COLS)
    return layout.astype(jnp.int32)


def draw_expert_id(key, part):
    return (routing_table(key) // CAP).astype(jnp.int32)


def draw_slot_index(key, part):
    return (routing_table(key) % CAP).astype(jnp.int32)


def levels(key, shape, cuts, least, high):
    factor_of = 1.0
    for position, blocks in cuts:
        steps = jax.random.uniform(jax.random.fold_in(jax.random.fold_in(key, 6), position), (blocks,), jnp.float32, least / len(cuts), high / len(cuts))
        factor_of = factor_of * jnp.repeat(jnp.exp(steps), shape[position] // blocks).reshape((-1,) + (1,) * (len(shape) - 1 - position))
    return factor_of


def noise(stream_key, shape, scale, bound, cuts=(), dtype=jnp.bfloat16):
    factor_of = levels(stream_key, shape, cuts, -0.22, 0.18) if cuts else 1.0
    drawn = jax.random.normal(stream_key, shape, jnp.float32) * scale * factor_of
    return jnp.minimum(jnp.maximum(drawn, -bound), bound).astype(dtype)


def setup_inputs(seed: int = 0) -> dict:
    key_of = jax.random.split(jax.random.key(seed), 13)
    return {
        "queries": draw_queries(jax.random.fold_in(key_of[12], 71), 0),
        "key_vectors": draw_key_vectors(jax.random.fold_in(key_of[12], 71), 0),
        "values": noise(key_of[2], (IMG_ROWS, IMG_COLS, D), 1.0, 6.0, ((0, 8), (1, 32))),
        "residual": draw_residual(jax.random.fold_in(key_of[12], 71), 0),
        "cotangent": noise(key_of[4], (IMG_ROWS, IMG_COLS, D), 1.0, 6.0, ((0, 8), (1, 32))),
        "out_proj": noise(key_of[5], (D, D), D ** -0.5, 0.25),
        "norm_gain": jnp.clip(1.0 + 0.1 * jax.random.normal(key_of[6], (D,), jnp.float32), 0.5, 1.5),
        "router": noise(key_of[7], (D, EXPERTS), D ** -0.5, 0.25),
        "expert_in": noise(key_of[8], (EXPERTS, D, HID), D ** -0.5, 0.25, ((0, 32),)),
        "expert_out": noise(key_of[9], (EXPERTS, HID, D), HID ** -0.5, 0.125, ((0, 32),)),
        "expert_id": draw_expert_id(jax.random.fold_in(key_of[12], 71), 0),
        "slot_index": draw_slot_index(jax.random.fold_in(key_of[12], 71), 0),
    }


EPSILON = 1e-05
NEGATIVE = -1e+30
GELU_COEF = 0.7978845608028654
CUBIC_COEF = 0.044715

def gelu_value(inputs):
    inner = GELU_COEF * (inputs + CUBIC_COEF * inputs * inputs * inputs)
    return 0.5 * inputs * (1.0 + jnp.tanh(inner))

def gelu_slope(inputs):
    tangent = jnp.tanh(GELU_COEF * (inputs + CUBIC_COEF * inputs * inputs * inputs))
    return 0.5 * (1.0 + tangent) + 0.5 * inputs * (1.0 - tangent * tangent) * GELU_COEF * (1.0 + 3.0 * CUBIC_COEF * inputs * inputs)

def lowered(array):
    return lax.optimization_barrier(array.astype(jnp.bfloat16))

def to_windows(image):
    channels = image.shape[-1]
    blocked = image.reshape(N_GY, WIN, N_GX, WIN, channels).transpose(0, 2, 1, 3, 4)
    return blocked.reshape(N_GY * N_GX, WIN * WIN, channels)

def from_windows(windows):
    channels = windows.shape[-1]
    blocked = windows.reshape(N_GY, N_GX, WIN, WIN, channels).transpose(0, 2, 1, 3, 4)
    return blocked.reshape(IMG_ROWS, IMG_COLS, channels)

def window_probs(win_query, win_key, win_label):
    query_heads = win_query.reshape(WIN * WIN, HEADS, HEAD_DIM).astype(jnp.float32)
    key_heads = win_key.reshape(WIN * WIN, HEADS, HEAD_DIM).astype(jnp.float32)
    scores = jnp.einsum('qhd,khd->hqk', query_heads, key_heads) * HEAD_DIM ** (-0.5)
    allowed = win_label[:, None] == win_label[None, :]
    return jax.nn.softmax(jnp.where(allowed[None], scores, NEGATIVE), axis=-1)

def reference(queries, key_vectors, values, residual, cotangent, out_proj, norm_gain, router, expert_in, expert_out, expert_id, slot_index):
    scale = HEAD_DIM ** (-0.5)
    tokens = WIN * WIN
    rolled = [to_windows(jnp.roll(image, (-SHIFT, -SHIFT), (0, 1))) for image in (queries, key_vectors, values)]
    row_pos = jnp.arange(IMG_ROWS)
    col_pos = jnp.arange(IMG_COLS)
    row_label = (row_pos >= IMG_ROWS - WIN).astype(jnp.int32) + (row_pos >= IMG_ROWS - SHIFT).astype(jnp.int32)
    col_label = (col_pos >= IMG_COLS - WIN).astype(jnp.int32) + (col_pos >= IMG_COLS - SHIFT).astype(jnp.int32)
    label_image = (3 * row_label[:, None] + col_label[None, :])[:, :, None]
    label_win = to_windows(label_image)[:, :, 0]

    def forward_window(operands):
        win_query, win_key, win_value, win_label = operands
        probs_low = lowered(window_probs(win_query, win_key, win_label))
        value_heads = win_value.reshape(tokens, HEADS, HEAD_DIM).astype(jnp.float32)
        mixed = jnp.einsum('hqk,khd->qhd', probs_low.astype(jnp.float32), value_heads)
        return mixed.reshape(tokens, D).astype(jnp.bfloat16)
    mixed_win = lax.map(forward_window, (rolled[0], rolled[1], rolled[2], label_win))
    mixed_flat = mixed_win.reshape(-1, D)
    attended = jnp.dot(mixed_flat, out_proj, preferred_element_type=jnp.float32).astype(jnp.bfloat16)
    attn_image = jnp.roll(from_windows(attended.reshape(-1, tokens, D)), (SHIFT, SHIFT), (0, 1))
    stream = (residual.astype(jnp.float32) + attn_image.astype(jnp.float32)).reshape(-1, D)
    centered = stream - lax.optimization_barrier(jnp.mean(stream, axis=-1, keepdims=True))
    inv_std = lax.rsqrt(lax.optimization_barrier(jnp.mean(centered * centered, axis=-1, keepdims=True)) + EPSILON)
    normed = centered * inv_std
    hidden_in = (normed * norm_gain).astype(jnp.bfloat16)
    experts_flat = expert_id.reshape(-1).astype(jnp.int32)
    logits_all = jnp.dot(hidden_in, router, preferred_element_type=jnp.float32)
    logit = jnp.take_along_axis(logits_all, experts_flat[:, None], axis=1)[:, 0]
    gate = jax.nn.sigmoid(logit)
    tile_row = jnp.broadcast_to((jnp.arange(IMG_ROWS) // WIN)[:, None], (IMG_ROWS, IMG_COLS))
    tile_col = jnp.broadcast_to((jnp.arange(IMG_COLS) // WIN)[None, :], (IMG_ROWS, IMG_COLS))
    place = (((expert_id * N_GY + tile_row) * N_GX + tile_col) * CAP + slot_index).reshape(-1).astype(jnp.int32)
    total_slots = EXPERTS * N_GY * N_GX * CAP
    cot_flat = cotangent.reshape(-1, D)
    buf_hidden = jnp.zeros((total_slots, D), jnp.bfloat16).at[place].set(hidden_in).reshape(EXPERTS, -1, D)
    buf_cot = jnp.zeros((total_slots, D), jnp.bfloat16).at[place].set(cot_flat).reshape(EXPERTS, -1, D)
    buf_gate = jnp.zeros((total_slots,), jnp.bfloat16).at[place].set(gate.astype(jnp.bfloat16)).reshape(EXPERTS, -1)

    def expert_pass(operands):
        slot_hidden, slot_cot, slot_gate, weight_in, weight_out = operands
        pre = jnp.dot(slot_hidden, weight_in, preferred_element_type=jnp.float32)
        activated = lowered(gelu_value(pre))
        produced = jnp.dot(activated, weight_out, preferred_element_type=jnp.float32)
        grad_gate_slot = lax.optimization_barrier(jnp.sum(slot_cot.astype(jnp.float32) * produced, axis=-1)).astype(jnp.bfloat16)
        scaled = lowered(slot_gate.astype(jnp.float32)[:, None] * slot_cot.astype(jnp.float32))
        grad_pre = lowered(jnp.dot(scaled, weight_out.T, preferred_element_type=jnp.float32) * gelu_slope(pre))
        grad_slot = jnp.dot(grad_pre, weight_in.T, preferred_element_type=jnp.float32).astype(jnp.bfloat16)
        rows_hidden = slot_hidden.reshape(N_GY, -1, D).astype(jnp.float32)
        rows_grad = grad_pre.reshape(N_GY, -1, HID).astype(jnp.float32)
        rows_act = activated.reshape(N_GY, -1, HID).astype(jnp.float32)
        rows_scaled = scaled.reshape(N_GY, -1, D).astype(jnp.float32)
        part_in = lowered(jnp.einsum('ird,irf->idf', rows_hidden, rows_grad))
        part_out = lowered(jnp.einsum('irf,ird->ifd', rows_act, rows_scaled))
        grad_in = lax.optimization_barrier(jnp.sum(part_in.astype(jnp.float32), axis=0)).astype(jnp.bfloat16)
        grad_out = lax.optimization_barrier(jnp.sum(part_out.astype(jnp.float32), axis=0)).astype(jnp.bfloat16)
        return (grad_slot, grad_gate_slot, grad_in, grad_out)
    grad_slots, grad_gates, grad_expert_in, grad_expert_out = lax.map(expert_pass, (buf_hidden, buf_cot, buf_gate, expert_in, expert_out))
    grad_gate_tok = grad_gates.reshape(-1)[place].astype(jnp.float32)
    grad_logit = grad_gate_tok * gate * (1.0 - gate)
    router_col = router.astype(jnp.float32).T[experts_flat]
    grad_hidden = grad_slots.reshape(-1, D)[place].astype(jnp.float32) + grad_logit[:, None] * router_col
    onehot = (experts_flat[:, None] == jnp.arange(EXPERTS)[None, :]).astype(jnp.float32)
    grad_router = jnp.dot(hidden_in.astype(jnp.float32).T, onehot * grad_logit[:, None], precision=lax.Precision.HIGHEST)
    grad_gain = lax.optimization_barrier(jnp.sum(grad_hidden * normed, axis=0))
    scaled_grad = grad_hidden * norm_gain
    stream_grad = cot_flat.astype(jnp.float32) + inv_std * (scaled_grad - lax.optimization_barrier(jnp.mean(scaled_grad, axis=-1, keepdims=True)) - normed * lax.optimization_barrier(jnp.mean(scaled_grad * normed, axis=-1, keepdims=True)))
    grad_input = stream_grad.astype(jnp.bfloat16).reshape(IMG_ROWS, IMG_COLS, D)
    grad_win = to_windows(jnp.roll(grad_input, (-SHIFT, -SHIFT), (0, 1))).reshape(-1, D)
    grad_out_proj = jnp.dot(mixed_flat.T, grad_win, preferred_element_type=jnp.float32).astype(jnp.bfloat16)
    grad_mixed = jnp.dot(grad_win, out_proj.T, preferred_element_type=jnp.float32).astype(jnp.bfloat16).reshape(-1, tokens, D)

    def backward_window(operands):
        win_query, win_key, win_value, win_label, grad_mixed_win = operands
        probs = window_probs(win_query, win_key, win_label)
        probs_low = lowered(probs)
        query_heads = win_query.reshape(tokens, HEADS, HEAD_DIM).astype(jnp.float32)
        key_heads = win_key.reshape(tokens, HEADS, HEAD_DIM).astype(jnp.float32)
        value_heads = win_value.reshape(tokens, HEADS, HEAD_DIM).astype(jnp.float32)
        grad_heads = grad_mixed_win.reshape(tokens, HEADS, HEAD_DIM).astype(jnp.float32)
        grad_val = jnp.einsum('hqk,qhd->khd', probs_low.astype(jnp.float32), grad_heads).astype(jnp.bfloat16)
        grad_probs = jnp.einsum('qhd,khd->hqk', grad_heads, value_heads)
        grad_scores = lowered(probs * (grad_probs - lax.optimization_barrier(jnp.sum(probs * grad_probs, axis=-1, keepdims=True))) * scale)
        grad_query = jnp.einsum('hqk,khd->qhd', grad_scores.astype(jnp.float32), key_heads).astype(jnp.bfloat16)
        grad_key = jnp.einsum('hqk,qhd->khd', grad_scores.astype(jnp.float32), query_heads).astype(jnp.bfloat16)
        return (grad_query.reshape(tokens, D), grad_key.reshape(tokens, D), grad_val.reshape(tokens, D))
    grad_query_win, grad_key_win, grad_val_win = lax.map(backward_window, (rolled[0], rolled[1], rolled[2], label_win, grad_mixed))
    grad_queries = jnp.roll(from_windows(grad_query_win), (SHIFT, SHIFT), (0, 1))
    grad_keys = jnp.roll(from_windows(grad_key_win), (SHIFT, SHIFT), (0, 1))
    grad_values = jnp.roll(from_windows(grad_val_win), (SHIFT, SHIFT), (0, 1))
    return (grad_queries, grad_keys, grad_values, grad_input, grad_out_proj, grad_gain, grad_router, grad_expert_in, grad_expert_out)
```

```python
import jax
import jax.numpy as jnp
from jax import lax
from jax.sharding import PartitionSpec as P

HEADS = 16
EPSILON = 1e-05
NEGATIVE = -1e30
GELU_COEF = 0.7978845608028654
CUBIC_COEF = 0.044715
AXES = ("gy", "gx")


def fetch(block, down, right):
    rows, cols = lax.axis_size("gy"), lax.axis_size("gx")
    if down == 0 and right == 0:
        return block
    if down == 0:
        return lax.ppermute(block, "gx", [((j + right) % cols, j) for j in range(cols)])
    if right == 0:
        return lax.ppermute(block, "gy", [((i + down) % rows, i) for i in range(rows)])
    route = [
        (((i + down) % rows) * cols + (j + right) % cols, i * cols + j)
        for i in range(rows)
        for j in range(cols)
    ]
    return lax.ppermute(block, AXES, route)


def to_quarters(tile):
    side, _, width = tile.shape
    half = side // 2
    return tile.reshape(2, half, 2, half, width).transpose(0, 2, 1, 3, 4).reshape(4, half * half, width)


def from_quarters(quarters, side):
    half = side // 2
    width = quarters[0].shape[-1]
    halves = [q.reshape(half, half, width) for q in quarters]
    return jnp.concatenate(
        (
            jnp.concatenate(halves[:2], axis=1),
            jnp.concatenate(halves[2:], axis=1),
        ),
        axis=0,
    )


def image_to_window(quarters):
    return [fetch(quarters[3 - p], p // 2, p % 2) for p in range(4)]


def window_to_image(pieces):
    return [fetch(pieces[3 - q], -((3 - q) // 2), -((3 - q) % 2)) for q in range(4)]


def gelu_parts(inputs):
    square = inputs * inputs
    tangent = jnp.tanh(GELU_COEF * inputs * (1.0 + CUBIC_COEF * square))
    value = 0.5 * inputs * (1.0 + tangent)
    slope = 0.5 * (1.0 + tangent) + 0.5 * inputs * (1.0 - tangent * tangent) * GELU_COEF * (
        1.0 + 3.0 * CUBIC_COEF * square
    )
    return value, slope


def shards(
    queries,
    key_vectors,
    values,
    residual,
    cotangent,
    out_proj,
    norm_gain,
    router,
    expert_in,
    expert_out,
    expert_id,
    slot_index,
):
    f32, bf16 = jnp.float32, jnp.bfloat16
    side = queries.shape[0]
    width = queries.shape[2]
    head_size = width // HEADS
    tokens = side * side
    expert_count = router.shape[1]
    local_experts = expert_in.shape[0]
    hidden = expert_in.shape[2]
    capacity = 2 * tokens // expert_count
    slots_total = expert_count * capacity
    grid_rows, grid_cols = lax.axis_size("gy"), lax.axis_size("gx")
    devices = grid_rows * grid_cols
    row, col = lax.axis_index("gy"), lax.axis_index("gx")
    scale = head_size ** (-0.5)
    hidden_slice = hidden // grid_rows

    stacked = jnp.concatenate(
        [to_quarters(queries), to_quarters(key_vectors), to_quarters(values)], axis=1
    )
    pieces = image_to_window([stacked[q] for q in range(4)])
    quarter = tokens // 4
    win_query, win_key, win_value = (
        jnp.concatenate([p[quarter * n : quarter * (n + 1)] for p in pieces], axis=0)
        .reshape(tokens, HEADS, head_size)
        for n in range(3)
    )

    place = to_quarters((expert_id * capacity + slot_index)[:, :, None]).reshape(tokens)
    onehot = (jnp.arange(slots_total)[:, None] == place[None, :]).astype(bf16)
    cot = to_quarters(cotangent).reshape(tokens, width)

    def dispatch(rows):
        slots = jnp.dot(onehot, rows, preferred_element_type=f32).astype(bf16)
        arrived = lax.all_to_all(slots, "gx", 0, 0, tiled=True)
        return (
            arrived.reshape(grid_cols, local_experts, capacity, width)
            .transpose(1, 0, 2, 3)
            .reshape(local_experts, grid_cols * capacity, width)
        )

    slot_cot = dispatch(cot)
    cot_rows = [fetch(slot_cot, shift, 0) for shift in range(grid_rows)]
    spread = jnp.einsum("erd,efd->erf", slot_cot, expert_out, preferred_element_type=f32)

    index = jnp.arange(tokens)
    row_half, col_half = index // (tokens // 2), (index // quarter) % 2
    allowed = ((row_half[:, None] == row_half[None, :]) | (row < grid_rows - 1)) & (
        (col_half[:, None] == col_half[None, :]) | (col < grid_cols - 1)
    )
    scores = jnp.einsum("qhd,khd->hqk", win_query, win_key, preferred_element_type=f32) * scale
    probs = jax.nn.softmax(jnp.where(allowed[None], scores, NEGATIVE), axis=-1)
    probs_low = probs.astype(bf16)
    mixed_win = (
        jnp.einsum("hqk,khd->qhd", probs_low, win_value, preferred_element_type=f32)
        .astype(bf16)
        .reshape(4, quarter, width)
    )
    mixed = jnp.concatenate(window_to_image([mixed_win[p] for p in range(4)]), axis=0)

    attended = jnp.dot(mixed, out_proj, preferred_element_type=f32).astype(bf16)
    stream = to_quarters(residual).reshape(tokens, width).astype(f32) + attended.astype(f32)
    centered = stream - jnp.mean(stream, axis=-1, keepdims=True)
    inv_std = lax.rsqrt(jnp.mean(centered * centered, axis=-1, keepdims=True) + EPSILON)
    normed = centered * inv_std
    hidden_in = (normed * norm_gain).astype(bf16)

    slot_hidden = dispatch(hidden_in)
    hidden_rows = [fetch(slot_hidden, shift, 0) for shift in range(grid_rows)]
    router_rows = lax.dynamic_slice_in_dim(router, col * local_experts, local_experts, 1).T.astype(f32)

    def gate_of(rows):
        logit = jnp.sum(rows.astype(f32) * router_rows[:, None, :], axis=-1)
        return jax.nn.sigmoid(logit)

    gate = gate_of(slot_hidden)
    gate_low = gate.astype(bf16).astype(f32)[:, :, None]
    pre = jnp.einsum("erd,edf->erf", slot_hidden, expert_in, preferred_element_type=f32)
    activated, slope = gelu_parts(pre)
    grad_gate = jnp.sum(activated * spread, axis=-1)
    grad_pre = (gate_low * spread * slope).astype(bf16)
    grad_slot = jnp.einsum("erf,edf->erd", grad_pre, expert_in, preferred_element_type=f32)
    grad_logit = (grad_gate * gate * (1.0 - gate))[:, :, None]
    grad_hidden_slot = grad_slot + grad_logit * router_rows[:, None, :]
    hidden_wide = slot_hidden.astype(f32)
    small = jnp.concatenate(
        (
            jnp.sum(hidden_wide * grad_logit, axis=1),
            jnp.sum(hidden_wide * grad_hidden_slot, axis=(0, 1))[None] / norm_gain[None],
        ),
        axis=0,
    )
    returning = (
        grad_hidden_slot.astype(bf16)
        .reshape(local_experts, grid_cols, capacity, width)
        .transpose(1, 0, 2, 3)
        .reshape(slots_total, width)
    )
    returned = lax.all_to_all(returning, "gx", 0, 0, tiled=True)

    grad_hidden = lax.dot_general(
        onehot, returned, (((0,), (0,)), ((), ())), preferred_element_type=f32
    )
    scaled_grad = grad_hidden * norm_gain
    stream_grad = cot.astype(f32) + inv_std * (
        scaled_grad
        - jnp.mean(scaled_grad, axis=-1, keepdims=True)
        - normed * jnp.mean(scaled_grad * normed, axis=-1, keepdims=True)
    )
    grad_input = stream_grad.astype(bf16)
    grad_mixed_image = lax.dot_general(
        grad_input, out_proj, (((1,), (1,)), ((), ())), preferred_element_type=f32
    ).astype(bf16)
    grad_mixed = jnp.concatenate(
        image_to_window([grad_mixed_image[quarter * q : quarter * (q + 1)] for q in range(4)]), axis=0
    ).reshape(tokens, HEADS, head_size)

    proj_part = lax.dot_general(
        mixed, grad_input, (((0,), (0,)), ((), ())), preferred_element_type=f32
    ).astype(bf16)
    tiles_down, tiles_across = width // 8, width // 128
    proj_tiles = (
        proj_part.reshape(tiles_down, 8, tiles_across, 128)
        .transpose(0, 2, 1, 3)
        .reshape(devices, -1, 128)
    )
    proj_arrived = lax.all_to_all(proj_tiles, AXES, 0, 0, tiled=True)
    proj_sum = jnp.sum(proj_arrived.astype(f32), axis=0).astype(bf16)

    distance = 1
    while distance < grid_rows:
        small = small + lax.ppermute(small, "gy", [(i ^ distance, i) for i in range(grid_rows)])
        distance *= 2
    share = lax.dynamic_index_in_dim(
        small.reshape(grid_rows, -1, 128 if small.size % (grid_rows * 128) == 0 else 1), row, 0, keepdims=False
    ).reshape(-1)
    pad = -share.size % 128
    share = jnp.pad(share, (0, pad)).reshape(-1, 128)
    high = share.astype(bf16)
    low = (share - high.astype(f32)).astype(bf16)
    outgoing = jnp.concatenate((proj_sum, high, low), axis=0)
    gathered = lax.all_to_all(
        jnp.broadcast_to(outgoing[None], (devices,) + outgoing.shape), AXES, 0, 0, tiled=True
    )
    proj_rows, small_rows = proj_sum.shape[0], high.shape[0]
    grad_proj = (
        gathered[:, :proj_rows]
        .reshape(tiles_down, tiles_across, 8, 128)
        .transpose(0, 2, 1, 3)
        .reshape(width, width)
    )
    smalls = gathered[:, proj_rows : proj_rows + small_rows].astype(f32) + gathered[
        :, proj_rows + small_rows :
    ].astype(f32)
    smalls = (
        smalls.reshape(grid_rows, grid_cols, -1)[:, :, : small.size // grid_rows]
        .transpose(1, 0, 2)
        .reshape(grid_cols, local_experts + 1, width)
    )
    grad_router = smalls[:, :local_experts].reshape(expert_count, width).T
    grad_gain = jnp.sum(smalls[:, local_experts], axis=0)

    grad_val = jnp.einsum("hqk,qhd->khd", probs_low, grad_mixed, preferred_element_type=f32).astype(bf16)
    grad_probs = jnp.einsum("qhd,khd->hqk", grad_mixed, win_value, preferred_element_type=f32)
    grad_scores = (
        probs * (grad_probs - jnp.sum(probs * grad_probs, axis=-1, keepdims=True)) * scale
    ).astype(bf16)
    grad_query = jnp.einsum("hqk,khd->qhd", grad_scores, win_key, preferred_element_type=f32).astype(bf16)
    grad_key = jnp.einsum("hqk,qhd->khd", grad_scores, win_query, preferred_element_type=f32).astype(bf16)
    grads = jnp.concatenate(
        [g.reshape(4, quarter, width) for g in (grad_query, grad_key, grad_val)], axis=1
    )
    image_grads = window_to_image([grads[p] for p in range(4)])
    image_out = [
        from_quarters([q[quarter * n : quarter * (n + 1)] for q in image_grads], side) for n in range(3)
    ]

    in_slice = lax.dynamic_slice_in_dim(expert_in, row * hidden_slice, hidden_slice, 2)
    out_slice = lax.dynamic_slice_in_dim(expert_out, row * hidden_slice, hidden_slice, 1)
    grad_in = jnp.zeros((local_experts, width, hidden_slice), f32)
    grad_out = jnp.zeros((local_experts, hidden_slice, width), f32)
    for rows_hidden, rows_cot in zip(hidden_rows, cot_rows):
        row_gate = gate_of(rows_hidden).astype(bf16).astype(f32)[:, :, None]
        row_pre = jnp.einsum("erd,edf->erf", rows_hidden, in_slice, preferred_element_type=f32)
        row_spread = jnp.einsum("erd,efd->erf", rows_cot, out_slice, preferred_element_type=f32)
        row_act, row_slope = gelu_parts(row_pre)
        row_grad_pre = (row_gate * row_spread * row_slope).astype(bf16)
        row_scaled = (row_gate * rows_cot.astype(f32)).astype(bf16)
        grad_in += jnp.einsum("erd,erf->edf", rows_hidden, row_grad_pre, preferred_element_type=f32)
        grad_out += jnp.einsum("erf,erd->efd", row_act.astype(bf16), row_scaled, preferred_element_type=f32)

    return (
        image_out[0],
        image_out[1],
        image_out[2],
        from_quarters([grad_input[quarter * q : quarter * (q + 1)] for q in range(4)], side),
        grad_proj,
        grad_gain,
        grad_router,
        grad_in.astype(bf16),
        grad_out.astype(bf16),
    )


def solution(mesh):
    tile = P("gy", "gx", None)
    return jax.shard_map(
        shards,
        mesh=mesh,
        in_specs=(tile,) * 5
        + (P(), P(), P(), P("gx", None, None), P("gx", None, None), P("gy", "gx"), P("gy", "gx")),
        out_specs=(tile,) * 4 + (P(), P(), P(), P("gx", None, "gy"), P("gx", "gy", None)),
        check_vma=False,
    )
```

```python
import functools

import jax
import jax.numpy as jnp
from jax import lax
from jax.experimental import pallas as pl
from jax.experimental.pallas import tpu as pltpu
from jax.sharding import Mesh
from jax.sharding import PartitionSpec as P

HEADS = 16
EPSILON = 1e-05
NEGATIVE = -1e30
GELU_COEF = 0.7978845608028654
CUBIC_COEF = 0.044715
GY = ("yh", "x")
GX = ("g", "c")
EVERY = GY + GX
ANY = pl.BlockSpec(memory_space=pl.ANY)


def fetch(block, down, right):
    rows, cols = lax.axis_size(GY), lax.axis_size(GX)
    if down == 0 and right == 0:
        return block
    if down == 0:
        return lax.ppermute(block, GX, [((j + right) % cols, j) for j in range(cols)])
    if right == 0:
        return lax.ppermute(block, GY, [((i + down) % rows, i) for i in range(rows)])
    route = [
        (((i + down) % rows) * cols + (j + right) % cols, i * cols + j)
        for i in range(rows)
        for j in range(cols)
    ]
    return lax.ppermute(block, EVERY, route)


def swap(block, axis):
    return lax.ppermute(block, axis, [(0, 1), (1, 0)])


def step(block, way):
    size = lax.axis_size("x")
    return lax.ppermute(block, "x", [(i, (i + way) % size) for i in range(size)])


def image_to_window(quarters):
    return [fetch(quarters[3 - p], p // 2, p % 2) for p in range(4)]


def window_to_image(pieces):
    return [fetch(pieces[3 - q], -((3 - q) // 2), -((3 - q) % 2)) for q in range(4)]


def gelu_parts(inputs):
    square = inputs * inputs
    tangent = jnp.tanh(GELU_COEF * inputs * (1.0 + CUBIC_COEF * square))
    value = 0.5 * inputs * (1.0 + tangent)
    slope = 0.5 * (1.0 + tangent) + 0.5 * inputs * (1.0 - tangent * tangent) * GELU_COEF * (
        1.0 + 3.0 * CUBIC_COEF * square
    )
    return value, slope

NN = (((1,), (0,)), ((), ()))
NT = (((1,), (1,)), ((), ()))
TN = (((0,), (0,)), ((), ()))
GROUP = 128


def mul(a, b, dims):
    return lax.dot_general(a, b, dims, preferred_element_type=jnp.float32)


def window_parts(pieces, quarter):
    return [
        jnp.concatenate([p[quarter * n : quarter * (n + 1), :] for p in pieces], axis=0) for n in range(3)
    ]


def attend_kernel(quarter, head_size, last_ref, *refs):
    pieces, mixed_refs, probs_ref = refs[:4], refs[-5:-1], refs[-1]
    query, key, value = window_parts(pieces, quarter)
    tokens = query.shape[0]
    of_key = lax.broadcasted_iota(jnp.int32, (tokens, tokens), 0)
    of_query = lax.broadcasted_iota(jnp.int32, (tokens, tokens), 1)
    differs = jnp.bitwise_xor(of_key // quarter, of_query // quarter)
    hidden = jnp.bitwise_and(differs, last_ref[0]) != 0
    scale = head_size ** (-0.5)
    lane_head = lax.broadcasted_iota(jnp.int32, query.shape, 1) // head_size
    value_t = value.T
    mixed_t = []
    for h in range(GROUP // head_size):
        masked = jnp.where(lane_head == h, query, jnp.zeros_like(query))
        scores = mul(key, masked, NT) * scale
        scores = jnp.where(hidden, NEGATIVE, scores)
        weights = jnp.exp(scores - jnp.max(scores, axis=0, keepdims=True))
        probs = (weights * (1.0 / jnp.sum(weights, axis=0, keepdims=True))).astype(jnp.bfloat16)
        probs_ref[h] = probs
        mixed_t.append(mul(value_t[h * head_size : (h + 1) * head_size, :], probs, NN))
    mixed = jnp.concatenate(mixed_t, axis=0).T.astype(jnp.bfloat16)
    for p in range(4):
        mixed_refs[p][...] = mixed[quarter * p : quarter * (p + 1), :]


def attend_back_kernel(quarter, head_size, *refs):
    pieces, grad_refs, probs_refs, outs = refs[:4], refs[4:8], refs[8:10], refs[-4:]
    front = pl.program_id(0) < pl.num_programs(0) // 2
    query, key, value = window_parts(pieces, quarter)
    grad = jnp.concatenate([r[...] for r in grad_refs], axis=0)
    scale = head_size ** (-0.5)
    lane_head = lax.broadcasted_iota(jnp.int32, query.shape, 1) // head_size
    key_t = key.T
    grad_query_t = []
    grad_key = jnp.zeros(query.shape, jnp.float32)
    grad_value = jnp.zeros(query.shape, jnp.float32)
    for h in range(GROUP // head_size):
        mine = lane_head == h
        masked_grad = jnp.where(mine, grad, jnp.zeros_like(grad))
        masked_query = jnp.where(mine, query, jnp.zeros_like(query))
        probs_low = jnp.where(front, probs_refs[0][h], probs_refs[1][h])
        probs = probs_low.astype(jnp.float32)
        grad_probs = mul(value, masked_grad, NT)
        total = jnp.sum(probs * grad_probs, axis=0, keepdims=True)
        grad_scores = (probs * (grad_probs - total) * scale).astype(jnp.bfloat16)
        grad_value += mul(probs_low, masked_grad, NN)
        grad_key += mul(grad_scores, masked_query, NN)
        grad_query_t.append(mul(key_t[h * head_size : (h + 1) * head_size, :], grad_scores, NN))
    grad_query = jnp.concatenate(grad_query_t, axis=0).T
    for n, g in enumerate((grad_query, grad_key, grad_value)):
        low = g.astype(jnp.bfloat16)
        for p in range(4):
            outs[p][quarter * n : quarter * (n + 1), :] = low[quarter * p : quarter * (p + 1), :]


def params(**more):
    return pltpu.CompilerParams(vmem_limit_bytes=16 * 1024 * 1024, **more)


def attend(last, pieces, quarter, head_size, part, earlier):
    tokens, width = 4 * quarter, pieces[0].shape[1] // 2
    heads, groups = GROUP // head_size, width // GROUP
    return pl.pallas_call(
        functools.partial(attend_kernel, quarter, head_size),
        grid=(groups,),
        in_specs=[pl.BlockSpec(memory_space=pltpu.SMEM)]
        + [pl.BlockSpec((3 * quarter, GROUP), lambda g: (0, g + part * groups))] * 4
        + [ANY] * len(earlier),
        out_specs=[pl.BlockSpec((quarter, GROUP), lambda g: (0, g))] * 4
        + [pl.BlockSpec((heads, tokens, tokens), lambda g: (g, 0, 0))],
        out_shape=[jax.ShapeDtypeStruct((quarter, width), jnp.bfloat16)] * 4
        + [jax.ShapeDtypeStruct((width // head_size, tokens, tokens), jnp.bfloat16)],
        compiler_params=params(),
        cost_estimate=pl.CostEstimate(
            flops=16 * tokens * tokens * width, bytes_accessed=12 * tokens * width, transcendentals=0
        ),
        name="attend",
    )(last, *pieces, *earlier)


def attend_back(pieces, grads, probs, quarter, head_size, earlier):
    tokens, width = 4 * quarter, pieces[0].shape[1]
    heads, groups = GROUP // head_size, width // GROUP
    return pl.pallas_call(
        functools.partial(attend_back_kernel, quarter, head_size),
        grid=(groups,),
        in_specs=[pl.BlockSpec((3 * quarter, GROUP), lambda g: (0, g))] * 4
        + [pl.BlockSpec((quarter, GROUP), lambda g: (0, g))] * 4
        + [
            pl.BlockSpec((heads, tokens, tokens), lambda g: (jnp.minimum(g, groups // 2 - 1), 0, 0)),
            pl.BlockSpec((heads, tokens, tokens), lambda g: (jnp.maximum(g - groups // 2, 0), 0, 0)),
        ]
        + [ANY] * len(earlier),
        out_specs=[pl.BlockSpec((3 * quarter, GROUP), lambda g: (0, g))] * 4,
        out_shape=[jax.ShapeDtypeStruct((3 * quarter, width), jnp.bfloat16)] * 4,
        compiler_params=params(),
        cost_estimate=pl.CostEstimate(
            flops=8 * tokens * tokens * width * 4, bytes_accessed=12 * tokens * width * 2, transcendentals=0
        ),
        name="attend_back",
    )(*pieces, *grads, *probs, *earlier)


def expert_kernel(chunks, hidden_ref, weight_ref, spread_ref, router_ref, gain_ref, *refs):
    back_ref, small_ref, total, gate_sum, gate_ref = refs[-5:]
    e, c = pl.program_id(0), pl.program_id(1)
    f32 = jnp.float32
    slots = hidden_ref[0]

    @pl.when(c == 0)
    def _():
        logit = jnp.sum(slots.astype(f32) * router_ref[0], axis=-1, keepdims=True)
        gate_ref[...] = 1.0 / (1.0 + jnp.exp(-logit))
        total[...] = jnp.zeros_like(total)
        gate_sum[...] = jnp.zeros_like(gate_sum)

    gate = gate_ref[...]
    gate_low = gate.astype(jnp.bfloat16).astype(f32)
    spread = spread_ref[0]
    activated, slope = gelu_parts(mul(slots, weight_ref[0], NN))
    gate_sum[...] += jnp.sum(activated * spread, axis=-1, keepdims=True)
    grad_pre = (gate_low * spread * slope).astype(jnp.bfloat16)
    total[...] += mul(grad_pre, weight_ref[0], NT)

    @pl.when(c == chunks - 1)
    def _():
        grad_logit = gate_sum[...] * gate * (1.0 - gate)
        grad_hidden = total[...] + grad_logit * router_ref[0]
        back_ref[0] = grad_hidden.astype(jnp.bfloat16)
        wide = slots.astype(f32)
        small_ref[0, 0:1, :] = jnp.sum(wide * grad_logit, axis=0, keepdims=True)
        small_ref[0, 1:2, :] = jnp.sum(wide * grad_hidden, axis=0, keepdims=True) / gain_ref[...]


def experts(slot_hidden, expert_in, spread, router_rows, norm_gain, earlier):
    count, slots, width = slot_hidden.shape
    hidden = expert_in.shape[2]
    chunk = min(hidden, 512)
    chunks = hidden // chunk
    return pl.pallas_call(
        functools.partial(expert_kernel, chunks),
        grid=(count, chunks),
        in_specs=[
            pl.BlockSpec((1, slots, width), lambda e, c: (e, 0, 0)),
            pl.BlockSpec((1, width, chunk), lambda e, c: (e, 0, c)),
            pl.BlockSpec((1, slots, chunk), lambda e, c: (e, 0, c)),
            pl.BlockSpec((1, 1, width), lambda e, c: (e, 0, 0)),
            pl.BlockSpec((1, width), lambda e, c: (0, 0)),
        ]
        + [ANY] * len(earlier),
        out_specs=[
            pl.BlockSpec((1, slots, width), lambda e, c: (e, 0, 0)),
            pl.BlockSpec((1, 2, width), lambda e, c: (e, 0, 0)),
        ],
        out_shape=[
            jax.ShapeDtypeStruct((count, slots, width), jnp.bfloat16),
            jax.ShapeDtypeStruct((count, 2, width), jnp.float32),
        ],
        scratch_shapes=[
            pltpu.VMEM((slots, width), jnp.float32),
            pltpu.VMEM((slots, 1), jnp.float32),
            pltpu.VMEM((slots, 1), jnp.float32),
        ],
        compiler_params=params(),
        cost_estimate=pl.CostEstimate(
            flops=8 * count * slots * width * hidden, bytes_accessed=8 * count * slots * hidden, transcendentals=0
        ),
        name="experts",
    )(slot_hidden, expert_in, spread, router_rows[:, None, :], norm_gain[None, :], *earlier)


def two_row_sums(hidden_refs, cot_refs, in_ref, out_ref, router_ref):
    f32, bf16 = jnp.float32, jnp.bfloat16
    slots = jnp.concatenate([r[0] for r in hidden_refs], axis=0)
    cot = jnp.concatenate([r[0] for r in cot_refs], axis=0)
    logit = jnp.sum(slots.astype(f32) * router_ref[0], axis=-1, keepdims=True)
    gate = (1.0 / (1.0 + jnp.exp(-logit))).astype(bf16).astype(f32)
    activated, slope = gelu_parts(mul(slots, in_ref[0], NN))
    scaled = (gate * cot.astype(f32)).astype(bf16)
    grad_pre = (mul(scaled, out_ref[0], NT) * slope).astype(bf16)
    return mul(slots, grad_pre, TN), mul(scaled, activated.astype(bf16), TN)


def far_kernel(units_ref, *refs):
    far_in_ref, far_out_ref, token_ref = refs[-3:]
    sum_in, sum_out = two_row_sums(refs[:2], refs[2:4], *refs[4:7])
    far_in_ref[0] = sum_in.astype(jnp.bfloat16)
    far_out_ref[0] = sum_out.astype(jnp.bfloat16)
    token_ref[...] = jnp.zeros_like(token_ref)


def near_kernel(units_ref, *refs):
    far_in_ref, far_out_ref = refs[7:9]
    up_ref, down_ref, own_ref, token_ref = refs[-4:]
    d = pl.program_id(1)
    sum_in, sum_out = two_row_sums(refs[:2], refs[2:4], *refs[4:7])
    token_ref[...] = jnp.zeros_like(token_ref)

    @pl.when(d == 0)
    def _():
        up_ref[0, 0] = (sum_in + far_in_ref[0].astype(jnp.float32)).astype(jnp.bfloat16)
        up_ref[1, 0] = sum_out.astype(jnp.bfloat16)

    @pl.when(d == 1)
    def _():
        down_ref[0, 0] = sum_in.astype(jnp.bfloat16)
        down_ref[1, 0] = (sum_out + far_out_ref[0].astype(jnp.float32)).astype(jnp.bfloat16)

    @pl.when(d == 2)
    def _():
        own_ref[0, 0] = sum_in
        own_ref[1, 0] = sum_out


def weight_sums(kernel, ways, hidden_rows, cot_rows, expert_in, expert_out, router_rows, arrived, earlier):
    count, slots, width = hidden_rows[0].shape
    along = lax.axis_size("x")
    part = expert_in.shape[2] // (2 * along)
    half, place = lax.axis_index("yh"), lax.axis_index("x")
    units = jnp.stack([half * along + (place + way) % along for way in ways]).astype(jnp.int32)
    tile = pl.BlockSpec((1, slots, width), lambda e, d, units: (e, 0, 0))
    piece = pl.BlockSpec((1, width, part), lambda e, d, units: (e, 0, 0))
    pair = pl.BlockSpec((2, 1, width, part), lambda e, d, units: (0, e, 0, 0))
    token = pl.BlockSpec((8, 128), lambda e, d, units: (0, 0))
    bf16, f32 = jnp.bfloat16, jnp.float32
    if len(ways) == 1:
        out_specs = [piece, piece, token]
        out_shape = [jax.ShapeDtypeStruct((count, width, part), bf16)] * 2
    else:
        out_specs = [pair, pair, pair, token]
        out_shape = [jax.ShapeDtypeStruct((2, count, width, part), t) for t in (bf16, bf16, f32)]
    return pl.pallas_call(
        kernel,
        grid_spec=pltpu.PrefetchScalarGridSpec(
            num_scalar_prefetch=1,
            grid=(count, len(ways)),
            in_specs=[tile] * 4
            + [
                pl.BlockSpec((1, width, part), lambda e, d, units: (e, 0, units[d])),
                pl.BlockSpec((1, part, width), lambda e, d, units: (e, units[d], 0)),
                pl.BlockSpec((1, 1, width), lambda e, d, units: (e, 0, 0)),
            ]
            + [piece] * len(arrived)
            + [ANY] * len(earlier),
            out_specs=out_specs,
        ),
        out_shape=out_shape + [jax.ShapeDtypeStruct((8, 128), f32)],
        compiler_params=params(),
        cost_estimate=pl.CostEstimate(
            flops=32 * len(ways) * count * slots * width * part,
            bytes_accessed=4 * len(ways) * count * slots * width,
            transcendentals=0,
        ),
        name="weight_sums",
    )(units, *hidden_rows, *cot_rows, expert_in, expert_out, router_rows[:, None, :], *arrived, *earlier)


def weight_total_kernel(own_ref, up_ref, down_ref, grad_in_ref, grad_out_ref):
    f32 = jnp.float32
    total = own_ref[:, 0] + up_ref[:, 0].astype(f32) + down_ref[:, 0].astype(f32)
    grad_in_ref[0] = total[0].astype(jnp.bfloat16)
    grad_out_ref[0] = total[1].T.astype(jnp.bfloat16)


def weight_total(own, up, down):
    _, count, width, part = own.shape
    arrived = pl.BlockSpec((2, 1, width, part), lambda e: (0, e, 0, 0))
    return pl.pallas_call(
        weight_total_kernel,
        grid=(count,),
        in_specs=[arrived] * 3,
        out_specs=[
            pl.BlockSpec((1, width, part), lambda e: (e, 0, 0)),
            pl.BlockSpec((1, part, width), lambda e: (e, 0, 0)),
        ],
        out_shape=[
            jax.ShapeDtypeStruct((count, width, part), jnp.bfloat16),
            jax.ShapeDtypeStruct((count, part, width), jnp.bfloat16),
        ],
        compiler_params=params(),
        name="weight_total",
    )(own, up, down)


def quarter_of(tile_ref, q):
    half = tile_ref.shape[0] // 2
    a, b = q // 2, q % 2
    block = tile_ref[half * a : half * (a + 1), half * b : half * (b + 1), :]
    return block.reshape(half * half, tile_ref.shape[2])


def quarters_kernel(count, *refs):
    for n in range(count):
        for q in range(4):
            block = quarter_of(refs[n], q)
            rows = block.shape[0]
            refs[count + q][rows * n : rows * (n + 1), :] = block


def quarters(tiles):
    side, _, width = tiles[0].shape
    return pl.pallas_call(
        functools.partial(quarters_kernel, len(tiles)),
        grid=(width // GROUP,),
        in_specs=[pl.BlockSpec((side, side, GROUP), lambda g: (0, 0, g))] * len(tiles),
        out_specs=[pl.BlockSpec((len(tiles) * side * side // 4, GROUP), lambda g: (0, g))] * 4,
        out_shape=[jax.ShapeDtypeStruct((len(tiles) * side * side // 4, width), tiles[0].dtype)] * 4,
        compiler_params=params(),
        name="quarters",
    )(*tiles)


def tiles_kernel(count, *refs):
    for n in range(count):
        tile_ref = refs[4 + n]
        half, width = tile_ref.shape[0] // 2, tile_ref.shape[2]
        for q in range(4):
            a, b = q // 2, q % 2
            block = refs[q][half * half * n : half * half * (n + 1), :].reshape(half, half, width)
            tile_ref[half * a : half * (a + 1), half * b : half * (b + 1), :] = block


def tiles(parts, count, side):
    width = parts[0].shape[1]
    return pl.pallas_call(
        functools.partial(tiles_kernel, count),
        grid=(width // GROUP,),
        in_specs=[pl.BlockSpec((parts[0].shape[0], GROUP), lambda g: (0, g))] * 4,
        out_specs=[pl.BlockSpec((side, side, GROUP), lambda g: (0, 0, g))] * count,
        out_shape=[jax.ShapeDtypeStruct((side, side, width), parts[0].dtype)] * count,
        compiler_params=params(),
        name="tiles",
    )(*parts)


def slot_picker(place_ref, slots):
    place = place_ref[...]
    index = lax.broadcasted_iota(jnp.int32, (slots, place.shape[1]), 0)
    return (index == place).astype(jnp.bfloat16)


def to_slots_kernel(place_ref, *refs):
    out_ref = refs[-1]
    rows = jnp.concatenate([r[...] for r in refs[:4]], axis=0)
    out_ref[...] = mul(slot_picker(place_ref, out_ref.shape[0]), rows, NN).astype(out_ref.dtype)


def to_slots(place, parts, slots, earlier):
    width = parts[0].shape[1]
    whole = pl.BlockSpec(memory_space=pltpu.VMEM)
    return pl.pallas_call(
        to_slots_kernel,
        in_specs=[whole] * 5 + [ANY] * len(earlier),
        out_shape=jax.ShapeDtypeStruct((slots, width), parts[0].dtype),
        compiler_params=params(),
        name="to_slots",
    )(place, *parts, *earlier)


def norm_kernel(place_ref, gain_ref, proj_ref, *refs):
    f32, bf16 = jnp.float32, jnp.bfloat16
    mixed_refs, residual_refs = refs[:4], refs[4:8]
    slots_ref, normed_ref, inv_ref = refs[8:]
    mixed = jnp.concatenate([r[...] for r in mixed_refs], axis=0)
    residual = jnp.concatenate([r[...] for r in residual_refs], axis=0)
    attended = mul(mixed, proj_ref[...], NN).astype(bf16)
    stream = residual.astype(f32) + attended.astype(f32)
    centered = stream - jnp.mean(stream, axis=-1, keepdims=True)
    inv_std = lax.rsqrt(jnp.mean(centered * centered, axis=-1, keepdims=True) + EPSILON)
    normed = centered * inv_std
    hidden_in = (normed * gain_ref[...]).astype(bf16)
    normed_ref[...] = normed
    inv_ref[...] = inv_std
    slots_ref[...] = mul(slot_picker(place_ref, slots_ref.shape[0]), hidden_in, NN).astype(bf16)


def norm(place, gain, out_proj, mixed, residual, slots):
    tokens, width = place.shape[1], out_proj.shape[0]
    return pl.pallas_call(
        norm_kernel,
        out_shape=[
            jax.ShapeDtypeStruct((slots, width), jnp.bfloat16),
            jax.ShapeDtypeStruct((tokens, width), jnp.float32),
            jax.ShapeDtypeStruct((tokens, 1), jnp.float32),
        ],
        compiler_params=params(),
        name="norm",
    )(place, gain, out_proj, *mixed, *residual)


def token_kernel(place_ref, gain_ref, proj_ref, returned_ref, normed_ref, inv_ref, *refs):
    f32, bf16 = jnp.float32, jnp.bfloat16
    mixed_refs, cot_refs = refs[:4], refs[4:8]
    grad_refs, grad_mixed_refs, part_ref = refs[-9:-5], refs[-5:-1], refs[-1]
    mixed = jnp.concatenate([r[...] for r in mixed_refs], axis=0)
    cot = jnp.concatenate([r[...] for r in cot_refs], axis=0)
    normed, inv_std = normed_ref[...], inv_ref[...]
    grad_hidden = mul(slot_picker(place_ref, returned_ref.shape[0]), returned_ref[...], TN)
    grad = grad_hidden * gain_ref[...]
    grad_input = (
        cot.astype(f32)
        + inv_std
        * (
            grad
            - jnp.mean(grad, axis=-1, keepdims=True)
            - normed * jnp.mean(grad * normed, axis=-1, keepdims=True)
        )
    ).astype(bf16)
    grad_mixed = mul(grad_input, proj_ref[...], NT).astype(bf16)
    part_ref[...] = mul(mixed, grad_input, TN).astype(bf16)
    quarter = grad_refs[0].shape[0]
    for q in range(4):
        grad_refs[q][...] = grad_input[quarter * q : quarter * (q + 1), :]
        grad_mixed_refs[q][...] = grad_mixed[quarter * q : quarter * (q + 1), :]


def token_grads(place, gain, out_proj, returned, normed, inv_std, mixed, cot, earlier):
    tokens, width = normed.shape
    whole = pl.BlockSpec(memory_space=pltpu.VMEM)
    return pl.pallas_call(
        token_kernel,
        in_specs=[whole] * 14 + [ANY] * len(earlier),
        out_shape=[jax.ShapeDtypeStruct((tokens // 4, width), jnp.bfloat16)] * 8
        + [jax.ShapeDtypeStruct((width, width), jnp.bfloat16)],
        compiler_params=params(),
        name="token_grads",
    )(place, gain, out_proj, returned, normed, inv_std, *mixed, *cot, *earlier)


def share_kernel(shares_ref, *refs):
    total = jnp.sum(shares_ref[...].astype(jnp.float32), axis=0, keepdims=True)
    refs[-1][...] = jnp.broadcast_to(total.astype(jnp.bfloat16), shares_ref.shape)


def pass_kernel(array_ref, *refs):
    refs[-1][...] = array_ref[...]


def after(array, earlier):
    whole = pl.BlockSpec(memory_space=pltpu.VMEM)
    return pl.pallas_call(
        pass_kernel,
        in_specs=[whole] + [ANY] * len(earlier),
        out_shape=jax.ShapeDtypeStruct(array.shape, array.dtype),
        compiler_params=params(),
        name="after",
    )(array, *earlier)


def share_sum(shares, earlier):
    whole = pl.BlockSpec(memory_space=pltpu.VMEM)
    return pl.pallas_call(
        share_kernel,
        in_specs=[whole] + [ANY] * len(earlier),
        out_shape=jax.ShapeDtypeStruct(shares.shape, shares.dtype),
        compiler_params=params(),
        name="share_sum",
    )(shares, *earlier)


def shards(
    queries,
    key_vectors,
    values,
    residual,
    cotangent,
    out_proj,
    norm_gain,
    router,
    expert_in,
    expert_out,
    expert_id,
    slot_index,
):
    f32, bf16 = jnp.float32, jnp.bfloat16
    side = queries.shape[0]
    width = queries.shape[2]
    head_size = width // HEADS
    tokens = side * side
    quarter = tokens // 4
    expert_count = router.shape[1]
    local_experts = expert_in.shape[0]
    capacity = 2 * tokens // expert_count
    slots_total = expert_count * capacity
    grid_rows, grid_cols = lax.axis_size(GY), lax.axis_size(GX)
    row, col = lax.axis_index(GY), lax.axis_index(GX)
    core = lax.axis_index("c")
    gain = norm_gain[None, :]

    own_pieces = quarters([queries, key_vectors, values])
    pieces = image_to_window(own_pieces)

    place = (
        (expert_id * capacity + slot_index)
        .reshape(2, side // 2, 2, side // 2)
        .transpose(0, 2, 1, 3)
        .reshape(1, tokens)
    )
    cot = quarters([cotangent])

    def exchange(slots):
        arrived = lax.all_to_all(slots, GX, 0, 0, tiled=True)
        return (
            arrived.reshape(grid_cols, local_experts, capacity, width)
            .transpose(1, 0, 2, 3)
            .reshape(local_experts, grid_cols * capacity, width)
        )

    slot_cot = exchange(to_slots(place, cot, slots_total, own_pieces[:1]))
    other_cot = swap(slot_cot, "yh")
    spread = jnp.einsum("erd,efd->erf", slot_cot, expert_out, preferred_element_type=f32)

    last = (2 * (row == grid_rows - 1) + (col == grid_cols - 1)).astype(jnp.int32)[None]
    front = attend(last, pieces, quarter, head_size, 0, ())
    back = attend(last, pieces, quarter, head_size, 1, (slot_cot,))
    mixed = window_to_image([jnp.concatenate((front[p], back[p]), axis=1) for p in range(4)])

    slots, normed, inv_std = norm(place, gain, out_proj, mixed, quarters([residual]), slots_total)

    slot_hidden = exchange(slots)
    other_hidden = swap(slot_hidden, "yh")
    router_rows = lax.dynamic_slice_in_dim(router, col * local_experts, local_experts, 1).T.astype(f32)
    grad_hidden_slot, small = experts(
        slot_hidden, expert_in, spread, router_rows, norm_gain, (other_cot,)
    )
    returning = (
        grad_hidden_slot.reshape(local_experts, grid_cols, capacity, width)
        .transpose(1, 0, 2, 3)
        .reshape(slots_total, width)
    )
    returned = lax.all_to_all(returning, GX, 0, 0, tiled=True)

    sums = functools.partial(
        weight_sums,
        hidden_rows=(slot_hidden, other_hidden),
        cot_rows=(slot_cot, other_cot),
        expert_in=expert_in,
        expert_out=expert_out,
        router_rows=router_rows,
    )
    far_in, far_out, far_done = sums(far_kernel, (2,), arrived=(), earlier=())
    far_in, far_out = step(far_in, 1), step(far_out, -1)

    outcome = token_grads(place, gain, out_proj, returned, normed, inv_std, mixed, cot, (far_done,))
    grad_input, grad_mixed_image, proj_part = outcome[:4], outcome[4:8], outcome[8]
    grad_mixed = image_to_window(grad_mixed_image)
    upward, downward, own_sums, near_done = sums(
        near_kernel, (1, -1, 0), arrived=(far_in, far_out), earlier=(grad_mixed_image[3],)
    )
    from_below, from_above = step(upward, 1), step(downward, -1)

    grads = attend_back(pieces, grad_mixed, (front[4], back[4]), quarter, head_size, (near_done,))

    router_table = lax.dynamic_update_slice(
        jnp.zeros((expert_count, width), bf16), small[:, 0].astype(bf16), (col * local_experts, 0)
    )
    gain_row = jnp.sum(small[:, 1], axis=0, keepdims=True).astype(bf16)
    table = jnp.concatenate(
        (proj_part, router_table, jnp.pad(gain_row, ((0, width // 8 - 1), (0, 0)))), axis=0
    )
    table_half = table.shape[0] // 2
    table = table.reshape(2, table_half, width)
    mine = lax.dynamic_index_in_dim(table, core, 0, keepdims=False)
    theirs = lax.dynamic_index_in_dim(table, 1 - core, 0, keepdims=False)
    paired = (mine.astype(f32) + swap(theirs, "c").astype(f32)).astype(bf16)
    peers = GY + ("g",)
    peer_count = lax.axis_size(peers)
    shares = lax.all_to_all(paired.reshape(peer_count, -1, 128), peers, 0, 0, tiled=True)
    summed = lax.all_to_all(share_sum(shares, grads[:1]), peers, 0, 0, tiled=True)
    image_out = tiles(window_to_image(grads), 3, side)
    summed = after(summed, image_out[:1]).reshape(table_half, width)
    sibling = swap(summed, "c")
    full = jnp.where(
        core == 0, jnp.concatenate((summed, sibling), axis=0), jnp.concatenate((sibling, summed), axis=0)
    )
    grad_proj = full[:width]
    grad_router = full[width : width + expert_count].T.astype(f32)
    grad_gain = full[width + expert_count].astype(f32)

    grad_in, grad_out = weight_total(own_sums, from_below, from_above)

    return (
        image_out[0],
        image_out[1],
        image_out[2],
        tiles(grad_input, 1, side)[0],
        grad_proj,
        grad_gain,
        grad_router,
        grad_in,
        grad_out,
    )


def solution(mesh):
    rows, cols = mesh.devices.shape
    split = Mesh(mesh.devices.reshape(2, rows // 2, cols // 2, 2), EVERY)
    tile = P(GY, GX, None)
    return jax.shard_map(
        shards,
        mesh=split,
        in_specs=(tile,) * 5 + (P(), P(), P(), P(GX, None, None), P(GX, None, None), P(GY, GX), P(GY, GX)),
        out_specs=(tile,) * 4 + (P(), P(), P(), P(GX, None, GY), P(GX, GY, None)),
        check_vma=False,
    )
```

```python
import functools

import jax
import jax.numpy as jnp
from jax import lax
from jax.experimental import pallas as pl
from jax.experimental.pallas import tpu as pltpu
from jax.sharding import Mesh
from jax.sharding import PartitionSpec as P

HEADS = 16
EPSILON = 1e-05
NEGATIVE = -1e30
GELU_COEF = 0.7978845608028654
CUBIC_COEF = 0.044715
GY = ("yh", "x")
GX = ("g", "c")
EVERY = GY + GX
ANY = pl.BlockSpec(memory_space=pl.ANY)
VMEM = pl.BlockSpec(memory_space=pltpu.VMEM)
SMEM = pl.BlockSpec(memory_space=pltpu.SMEM)


def fetch(block, down, right):
    rows, cols = lax.axis_size(GY), lax.axis_size(GX)
    if down == 0 and right == 0:
        return block
    if down == 0:
        return lax.ppermute(block, GX, [((j + right) % cols, j) for j in range(cols)])
    if right == 0:
        return lax.ppermute(block, GY, [((i + down) % rows, i) for i in range(rows)])
    route = [
        (((i + down) % rows) * cols + (j + right) % cols, i * cols + j)
        for i in range(rows)
        for j in range(cols)
    ]
    return lax.ppermute(block, EVERY, route)


def swap(block, axis):
    return lax.ppermute(block, axis, [(0, 1), (1, 0)])


def step(block, way):
    size = lax.axis_size("x")
    return lax.ppermute(block, "x", [(i, (i + way) % size) for i in range(size)])


def image_to_window(quarters):
    return [fetch(quarters[3 - p], p // 2, p % 2) for p in range(4)]


def window_to_image(pieces):
    return [fetch(pieces[3 - q], -((3 - q) // 2), -((3 - q) % 2)) for q in range(4)]


def gelu_parts(inputs):
    square = inputs * inputs
    tangent = jnp.tanh(GELU_COEF * inputs * (1.0 + CUBIC_COEF * square))
    value = 0.5 * inputs * (1.0 + tangent)
    slope = 0.5 * (1.0 + tangent) + 0.5 * inputs * (1.0 - tangent * tangent) * GELU_COEF * (
        1.0 + 3.0 * CUBIC_COEF * square
    )
    return value, slope

NN = (((1,), (0,)), ((), ()))
NT = (((1,), (1,)), ((), ()))
TN = (((0,), (0,)), ((), ()))
GROUP = 128


def mul(a, b, dims):
    return lax.dot_general(a, b, dims, preferred_element_type=jnp.float32)


def window_parts(pieces, quarter):
    return [
        jnp.concatenate([p[quarter * n : quarter * (n + 1), :] for p in pieces], axis=0) for n in range(3)
    ]


def attend_kernel(quarter, head_size, last_ref, *refs):
    pieces, mixed_refs, probs_ref = refs[:4], refs[-5:-1], refs[-1]
    query, key, value = window_parts(pieces, quarter)
    tokens = query.shape[0]
    of_key = lax.broadcasted_iota(jnp.int32, (tokens, tokens), 0)
    of_query = lax.broadcasted_iota(jnp.int32, (tokens, tokens), 1)
    differs = jnp.bitwise_xor(of_key // quarter, of_query // quarter)
    hidden = jnp.bitwise_and(differs, last_ref[0]) != 0
    scale = head_size ** (-0.5)
    lane_head = lax.broadcasted_iota(jnp.int32, query.shape, 1) // head_size
    value_t = value.T
    mixed_t = []
    for h in range(GROUP // head_size):
        masked = jnp.where(lane_head == h, query, jnp.zeros_like(query))
        scores = mul(key, masked, NT) * scale
        scores = jnp.where(hidden, NEGATIVE, scores)
        weights = jnp.exp(scores - jnp.max(scores, axis=0, keepdims=True))
        probs = (weights * (1.0 / jnp.sum(weights, axis=0, keepdims=True))).astype(jnp.bfloat16)
        probs_ref[h] = probs
        mixed_t.append(mul(value_t[h * head_size : (h + 1) * head_size, :], probs, NN))
    mixed = jnp.concatenate(mixed_t, axis=0).T.astype(jnp.bfloat16)
    for p in range(4):
        mixed_refs[p][...] = mixed[quarter * p : quarter * (p + 1), :]


def attend_back_kernel(quarter, head_size, *refs):
    pieces, grad_refs, probs_refs, outs = refs[:4], refs[4:8], refs[8:10], refs[-4:]
    front = pl.program_id(0) < pl.num_programs(0) // 2
    query, key, value = window_parts(pieces, quarter)
    grad = jnp.concatenate([r[...] for r in grad_refs], axis=0)
    scale = head_size ** (-0.5)
    lane_head = lax.broadcasted_iota(jnp.int32, query.shape, 1) // head_size
    key_t = key.T
    grad_query_t = []
    grad_key = jnp.zeros(query.shape, jnp.float32)
    grad_value = jnp.zeros(query.shape, jnp.float32)
    for h in range(GROUP // head_size):
        mine = lane_head == h
        masked_grad = jnp.where(mine, grad, jnp.zeros_like(grad))
        masked_query = jnp.where(mine, query, jnp.zeros_like(query))
        probs_low = jnp.where(front, probs_refs[0][h], probs_refs[1][h])
        probs = probs_low.astype(jnp.float32)
        grad_probs = mul(value, masked_grad, NT)
        total = jnp.sum(probs * grad_probs, axis=0, keepdims=True)
        grad_scores = (probs * (grad_probs - total) * scale).astype(jnp.bfloat16)
        grad_value += mul(probs_low, masked_grad, NN)
        grad_key += mul(grad_scores, masked_query, NN)
        grad_query_t.append(mul(key_t[h * head_size : (h + 1) * head_size, :], grad_scores, NN))
    grad_query = jnp.concatenate(grad_query_t, axis=0).T
    for n, g in enumerate((grad_query, grad_key, grad_value)):
        low = g.astype(jnp.bfloat16)
        for p in range(4):
            outs[p][quarter * n : quarter * (n + 1), :] = low[quarter * p : quarter * (p + 1), :]


def staged(kernel, count, *refs):
    inputs, (buffers, sems) = refs[:count], (refs[-1 - count : -1], refs[-1])
    copies = [pltpu.make_async_copy(inputs[n], buffers[n], sems.at[n]) for n in range(count)]
    for copy in copies:
        copy.start()
    for copy in copies:
        copy.wait()
    kernel(*buffers, *refs[count : -1 - count])


def on_staged(kernel, inputs, earlier, out_shape, name, flops=0):
    return pl.pallas_call(
        functools.partial(staged, kernel, len(inputs)),
        in_specs=[ANY] * (len(inputs) + len(earlier)),
        out_shape=out_shape,
        scratch_shapes=[pltpu.VMEM(x.shape, x.dtype) for x in inputs]
        + [pltpu.SemaphoreType.DMA((len(inputs),))],
        compiler_params=params(),
        cost_estimate=pl.CostEstimate(flops=flops, bytes_accessed=1, transcendentals=0),
        name=name,
    )(*inputs, *earlier)


def params():
    return pltpu.CompilerParams(vmem_limit_bytes=60 * 1024 * 1024)


def attend(last, pieces, quarter, head_size, part, earlier):
    tokens, width = 4 * quarter, pieces[0].shape[1] // 2
    heads, groups = GROUP // head_size, width // GROUP
    return pl.pallas_call(
        functools.partial(attend_kernel, quarter, head_size),
        grid=(groups,),
        in_specs=[SMEM]
        + [pl.BlockSpec((3 * quarter, GROUP), lambda g: (0, g + part * groups))] * 4
        + [ANY] * len(earlier),
        out_specs=[pl.BlockSpec((quarter, GROUP), lambda g: (0, g))] * 4
        + [pl.BlockSpec((heads, tokens, tokens), lambda g: (g, 0, 0))],
        out_shape=[jax.ShapeDtypeStruct((quarter, width), jnp.bfloat16)] * 4
        + [jax.ShapeDtypeStruct((width // head_size, tokens, tokens), jnp.bfloat16)],
        compiler_params=params(),
        cost_estimate=pl.CostEstimate(
            flops=16 * tokens * tokens * width, bytes_accessed=12 * tokens * width, transcendentals=0
        ),
        name="attend",
    )(last, *pieces, *earlier)


def attend_back(pieces, grads, probs, quarter, head_size, earlier):
    tokens, width = 4 * quarter, pieces[0].shape[1]
    heads, groups = GROUP // head_size, width // GROUP
    return pl.pallas_call(
        functools.partial(attend_back_kernel, quarter, head_size),
        grid=(groups,),
        in_specs=[pl.BlockSpec((3 * quarter, GROUP), lambda g: (0, g))] * 4
        + [pl.BlockSpec((quarter, GROUP), lambda g: (0, g))] * 4
        + [
            pl.BlockSpec((heads, tokens, tokens), lambda g: (jnp.minimum(g, groups // 2 - 1), 0, 0)),
            pl.BlockSpec((heads, tokens, tokens), lambda g: (jnp.maximum(g - groups // 2, 0), 0, 0)),
        ]
        + [ANY] * len(earlier),
        out_specs=[pl.BlockSpec((3 * quarter, GROUP), lambda g: (0, g))] * 4,
        out_shape=[jax.ShapeDtypeStruct((3 * quarter, width), jnp.bfloat16)] * 4,
        compiler_params=params(),
        cost_estimate=pl.CostEstimate(
            flops=8 * tokens * tokens * width * 4, bytes_accessed=12 * tokens * width * 2, transcendentals=0
        ),
        name="attend_back",
    )(*pieces, *grads, *probs, *earlier)


def bring(sources, buffers, sems):
    copies = [pltpu.make_async_copy(s, b, sems.at[n]) for n, (s, b) in enumerate(zip(sources, buffers))]
    for copy in copies:
        copy.start()
    return copies


def expert_kernel(chunk, hidden_hbm, cot_hbm, router_hbm, gain_hbm, in_hbm, out_hbm, *refs):
    back_ref, small_ref, ins, outs, sems, hidden_ref, cot_ref, router_ref, gain_ref, few_sems = refs
    f32 = jnp.float32
    count, chunks = ins.shape[:2]
    few = bring(
        (hidden_hbm, router_hbm, cot_hbm, gain_hbm), (hidden_ref, router_ref, cot_ref, gain_ref), few_sems
    )
    copies = {}
    for e in range(count):
        for c in range(chunks):
            units = pl.ds(chunk * c, chunk)
            copies[e, c] = (
                pltpu.make_async_copy(in_hbm.at[e, :, units], ins.at[e, c], sems.at[0, e, c]),
                pltpu.make_async_copy(out_hbm.at[e, units, :], outs.at[e, c], sems.at[1, e, c]),
            )
            for copy in copies[e, c]:
                copy.start()
    for copy in few:
        copy.wait()
    for e in range(count):
        slots = hidden_ref[e]
        wide = slots.astype(f32)
        router_row = router_ref[e]
        logit = jnp.sum(wide * router_row, axis=-1, keepdims=True)
        gate = 1.0 / (1.0 + jnp.exp(-logit))
        gate_low = gate.astype(jnp.bfloat16).astype(f32)
        total, gate_sum = 0.0, 0.0
        for c in range(chunks):
            for copy in copies[e, c]:
                copy.wait()
            weight, spread = ins[e, c], mul(cot_ref[e], outs[e, c], NT)
            activated, slope = gelu_parts(mul(slots, weight, NN))
            gate_sum += jnp.sum(activated * spread, axis=-1, keepdims=True)
            total += mul((gate_low * spread * slope).astype(jnp.bfloat16), weight, NT)
        grad_logit = gate_sum * gate * (1.0 - gate)
        grad_hidden = total + grad_logit * router_row
        back_ref[e] = grad_hidden.astype(jnp.bfloat16)
        small_ref[e, 0:1, :] = jnp.sum(wide * grad_logit, axis=0, keepdims=True)
        small_ref[e, 1:2, :] = jnp.sum(wide * grad_hidden, axis=0, keepdims=True) / gain_ref[...]


def experts(slot_hidden, slot_cot, expert_in, expert_out, router_rows, gain):
    count, slots, width = slot_hidden.shape
    hidden = expert_in.shape[2]
    chunk = min(hidden, 512)
    chunks = hidden // chunk
    return pl.pallas_call(
        functools.partial(expert_kernel, chunk),
        in_specs=[ANY] * 6,
        out_shape=[
            jax.ShapeDtypeStruct((count, slots, width), jnp.bfloat16),
            jax.ShapeDtypeStruct((count, 2, width), jnp.float32),
        ],
        scratch_shapes=[
            pltpu.VMEM((count, chunks, width, chunk), jnp.bfloat16),
            pltpu.VMEM((count, chunks, chunk, width), jnp.bfloat16),
            pltpu.SemaphoreType.DMA((2, count, chunks)),
            pltpu.VMEM(slot_hidden.shape, slot_hidden.dtype),
            pltpu.VMEM(slot_cot.shape, slot_cot.dtype),
            pltpu.VMEM(router_rows.shape, router_rows.dtype),
            pltpu.VMEM(gain.shape, gain.dtype),
            pltpu.SemaphoreType.DMA((4,)),
        ],
        compiler_params=params(),
        cost_estimate=pl.CostEstimate(
            flops=12 * count * slots * width * hidden, bytes_accessed=8 * count * slots * hidden, transcendentals=0
        ),
        name="experts",
    )(slot_hidden, slot_cot, router_rows, gain, expert_in, expert_out)


def weights_kernel(units_ref, *refs):
    f32, bf16 = jnp.float32, jnp.bfloat16
    in_hbm, out_hbm = refs[3:5]
    far_in_ref, far_out_ref, up_ref, down_ref, own_ref, token_ref, ins, outs, sems = refs[-13:-4]
    hidden_ref, cot_ref, router_ref = refs[-4:-1]
    few = bring(refs[:3], refs[-4:-1], refs[-1])
    count, ways, width, part = ins.shape
    copies = {}
    for e in range(count):
        for d in range(ways):
            units = pl.ds(pl.multiple_of(units_ref[d] * part, part), part)
            copies[e, d] = (
                pltpu.make_async_copy(in_hbm.at[e, :, units], ins.at[e, d], sems.at[0, e, d]),
                pltpu.make_async_copy(out_hbm.at[e, units, :], outs.at[e, d], sems.at[1, e, d]),
            )
            for copy in copies[e, d]:
                copy.start()
    token_ref[...] = jnp.zeros_like(token_ref)
    for copy in few:
        copy.wait()
    for e in range(count):
        slots = jnp.concatenate((hidden_ref[0, e], hidden_ref[1, e]), axis=0)
        cot = jnp.concatenate((cot_ref[0, e], cot_ref[1, e]), axis=0)
        logit = jnp.sum(slots.astype(f32) * router_ref[e], axis=-1, keepdims=True)
        gate = (1.0 / (1.0 + jnp.exp(-logit))).astype(bf16).astype(f32)
        scaled = (gate * cot.astype(f32)).astype(bf16)
        slots_t, scaled_t = slots.T, scaled.T
        for d in range(ways):
            for copy in copies[e, d]:
                copy.wait()
            activated, slope = gelu_parts(mul(slots, ins[e, d], NN))
            grad_pre = (mul(scaled, outs[e, d], NT) * slope).astype(bf16)
            sum_in = mul(slots_t, grad_pre, NN)
            sum_out = mul(scaled_t, activated.astype(bf16), NN)
            if d == 0:
                far_in_ref[e] = sum_in.astype(bf16)
                far_out_ref[e] = sum_out.astype(bf16)
            else:
                target = (up_ref, down_ref, own_ref)[d - 1]
                target[0, e] = sum_in.astype(target.dtype)
                target[1, e] = sum_out.astype(target.dtype)


def weight_sums(hidden_pair, cot_pair, router_rows, expert_in, expert_out, earlier):
    _, count, slots, width = hidden_pair.shape
    along = lax.axis_size("x")
    part = expert_in.shape[2] // (2 * along)
    half, place = lax.axis_index("yh"), lax.axis_index("x")
    units = jnp.stack([half * along + (place + way) % along for way in (2, 1, -1, 0)]).astype(jnp.int32)
    bf16, f32 = jnp.bfloat16, jnp.float32
    return pl.pallas_call(
        weights_kernel,
        in_specs=[SMEM] + [ANY] * (5 + len(earlier)),
        out_shape=[jax.ShapeDtypeStruct((count, width, part), bf16)] * 2
        + [jax.ShapeDtypeStruct((2, count, width, part), t) for t in (bf16, bf16, f32)]
        + [jax.ShapeDtypeStruct((8, 128), f32)],
        scratch_shapes=[
            pltpu.VMEM((count, 4, width, part), bf16),
            pltpu.VMEM((count, 4, part, width), bf16),
            pltpu.SemaphoreType.DMA((2, count, 4)),
        ]
        + [pltpu.VMEM(hidden_pair.shape, bf16)] * 2
        + [pltpu.VMEM(router_rows.shape, f32), pltpu.SemaphoreType.DMA((3,))],
        compiler_params=params(),
        cost_estimate=pl.CostEstimate(
            flops=128 * count * slots * width * part, bytes_accessed=16 * count * slots * width, transcendentals=0
        ),
        name="weight_sums",
    )(units, hidden_pair, cot_pair, router_rows, expert_in, expert_out, *earlier)


def join_kernel(up_ref, down_ref, far_in_ref, far_out_ref, up_out, down_out):
    f32, bf16 = jnp.float32, jnp.bfloat16
    up_out[0] = (up_ref[0].astype(f32) + far_in_ref[...].astype(f32)).astype(bf16)
    up_out[1] = up_ref[1]
    down_out[0] = down_ref[0]
    down_out[1] = (down_ref[1].astype(f32) + far_out_ref[...].astype(f32)).astype(bf16)


def join(up, down, far_in, far_out):
    return on_staged(
        join_kernel,
        (up, down, far_in, far_out),
        (),
        [jax.ShapeDtypeStruct(up.shape, up.dtype)] * 2,
        "join",
    )


def weight_total_kernel(own_ref, up_ref, down_ref, grad_in_ref, grad_out_ref):
    f32 = jnp.float32
    total = own_ref[:, 0] + up_ref[:, 0].astype(f32) + down_ref[:, 0].astype(f32)
    grad_in_ref[0] = total[0].astype(jnp.bfloat16)
    grad_out_ref[0] = total[1].T.astype(jnp.bfloat16)


def weight_total(own, up, down):
    _, count, width, part = own.shape
    arrived = pl.BlockSpec((2, 1, width, part), lambda e: (0, e, 0, 0))
    return pl.pallas_call(
        weight_total_kernel,
        grid=(count,),
        in_specs=[arrived] * 3,
        out_specs=[
            pl.BlockSpec((1, width, part), lambda e: (e, 0, 0)),
            pl.BlockSpec((1, part, width), lambda e: (e, 0, 0)),
        ],
        out_shape=[
            jax.ShapeDtypeStruct((count, width, part), jnp.bfloat16),
            jax.ShapeDtypeStruct((count, part, width), jnp.bfloat16),
        ],
        compiler_params=params(),
        name="weight_total",
    )(own, up, down)


def quarter_of(tile_ref, q):
    half = tile_ref.shape[0] // 2
    a, b = q // 2, q % 2
    block = tile_ref[half * a : half * (a + 1), half * b : half * (b + 1), :]
    return block.reshape(half * half, tile_ref.shape[2])


def quarters_kernel(count, *refs):
    outs, (buffer, sems) = refs[count : count + 4], refs[-2:]
    copies = [pltpu.make_async_copy(refs[n], buffer.at[n], sems.at[n]) for n in range(count)]
    for copy in copies:
        copy.start()
    for n in range(count):
        copies[n].wait()
        for q in range(4):
            block = quarter_of(buffer.at[n], q)
            rows = block.shape[0]
            outs[q][rows * n : rows * (n + 1), :] = block


def quarters(tiles):
    side, _, width = tiles[0].shape
    count = len(tiles)
    return pl.pallas_call(
        functools.partial(quarters_kernel, count),
        in_specs=[ANY] * count,
        out_shape=[jax.ShapeDtypeStruct((count * side * side // 4, width), tiles[0].dtype)] * 4,
        scratch_shapes=[
            pltpu.VMEM((count, side, side, width), tiles[0].dtype),
            pltpu.SemaphoreType.DMA((count,)),
        ],
        compiler_params=params(),
        name="quarters",
    )(*tiles)


def tiles_kernel(count, *refs):
    for n in range(count):
        tile_ref = refs[4 + n]
        half, width = tile_ref.shape[0] // 2, tile_ref.shape[2]
        for q in range(4):
            a, b = q // 2, q % 2
            block = refs[q][half * half * n : half * half * (n + 1), :].reshape(half, half, width)
            tile_ref[half * a : half * (a + 1), half * b : half * (b + 1), :] = block


def tiles(parts, count, side):
    width = parts[0].shape[1]
    return pl.pallas_call(
        functools.partial(tiles_kernel, count),
        grid=(width // GROUP,),
        in_specs=[pl.BlockSpec((parts[0].shape[0], GROUP), lambda g: (0, g))] * 4,
        out_specs=[pl.BlockSpec((side, side, GROUP), lambda g: (0, 0, g))] * count,
        out_shape=[jax.ShapeDtypeStruct((side, side, width), parts[0].dtype)] * count,
        compiler_params=params(),
        name="tiles",
    )(*parts)


def slot_picker(place_ref, slots):
    place = place_ref[...]
    index = lax.broadcasted_iota(jnp.int32, (slots, place.shape[1]), 0)
    return (index == place).astype(jnp.bfloat16)


def to_slots_kernel(place_ref, cot_hbm, residual_hbm, *refs):
    slots_ref, cot_ref, residual_ref, buffer, sems = refs[-5:]
    copies = [
        pltpu.make_async_copy(hbm, buffer.at[n], sems.at[n]) for n, hbm in enumerate((cot_hbm, residual_hbm))
    ]
    for copy in copies:
        copy.start()
    for n, out in enumerate((cot_ref, residual_ref)):
        copies[n].wait()
        for q in range(4):
            block = quarter_of(buffer.at[n], q)
            rows = block.shape[0]
            out[rows * q : rows * (q + 1), :] = block
        if n == 0:
            picker = slot_picker(place_ref, slots_ref.shape[0])
            slots_ref[...] = mul(picker, cot_ref[...], NN).astype(slots_ref.dtype)


def to_slots(place, cotangent, residual, slots, earlier):
    side, _, width = cotangent.shape
    low = cotangent.dtype
    return pl.pallas_call(
        to_slots_kernel,
        in_specs=[VMEM, ANY, ANY] + [ANY] * len(earlier),
        out_shape=[jax.ShapeDtypeStruct((slots, width), low)]
        + [jax.ShapeDtypeStruct((side * side, width), low)] * 2,
        scratch_shapes=[pltpu.VMEM((2, side, side, width), low), pltpu.SemaphoreType.DMA((2,))],
        compiler_params=params(),
        name="to_slots",
    )(place, cotangent, residual, *earlier)


def norm_kernel(place_ref, gain_ref, proj_ref, *refs):
    f32, bf16 = jnp.float32, jnp.bfloat16
    mixed_refs = refs[:4]
    residual_ref, slots_ref, normed_ref, inv_ref = refs[4], *refs[-3:]
    mixed = jnp.concatenate([r[...] for r in mixed_refs], axis=0)
    attended = mul(mixed, proj_ref[...], NN).astype(bf16)
    stream = residual_ref[...].astype(f32) + attended.astype(f32)
    centered = stream - jnp.mean(stream, axis=-1, keepdims=True)
    inv_std = lax.rsqrt(jnp.mean(centered * centered, axis=-1, keepdims=True) + EPSILON)
    normed = centered * inv_std
    hidden_in = (normed * gain_ref[...]).astype(bf16)
    normed_ref[...] = normed
    inv_ref[...] = inv_std
    slots_ref[...] = mul(slot_picker(place_ref, slots_ref.shape[0]), hidden_in, NN).astype(bf16)


def norm(place, gain, out_proj, mixed, residual, slots, earlier):
    tokens, width = place.shape[1], out_proj.shape[0]
    return on_staged(
        norm_kernel,
        (place, gain, out_proj, *mixed, residual),
        earlier,
        [
            jax.ShapeDtypeStruct((slots, width), jnp.bfloat16),
            jax.ShapeDtypeStruct((tokens, width), jnp.float32),
            jax.ShapeDtypeStruct((tokens, 1), jnp.float32),
        ],
        "norm",
    )


def token_kernel(place_ref, gain_ref, proj_ref, returned_ref, normed_ref, inv_ref, *refs):
    f32, bf16 = jnp.float32, jnp.bfloat16
    mixed_refs, cot_ref = refs[:4], refs[4]
    grad_refs, grad_mixed_refs, part_ref = refs[-9:-5], refs[-5:-1], refs[-1]
    mixed = jnp.concatenate([r[...] for r in mixed_refs], axis=0)
    cot = cot_ref[...]
    normed, inv_std = normed_ref[...], inv_ref[...]
    grad_hidden = mul(slot_picker(place_ref, returned_ref.shape[0]), returned_ref[...], TN)
    grad = grad_hidden * gain_ref[...]
    grad_input = (
        cot.astype(f32)
        + inv_std
        * (
            grad
            - jnp.mean(grad, axis=-1, keepdims=True)
            - normed * jnp.mean(grad * normed, axis=-1, keepdims=True)
        )
    ).astype(bf16)
    grad_mixed = mul(grad_input, proj_ref[...], NT).astype(bf16)
    part_ref[...] = mul(mixed, grad_input, TN).astype(bf16)
    quarter = grad_refs[0].shape[0]
    for q in range(4):
        grad_refs[q][...] = grad_input[quarter * q : quarter * (q + 1), :]
        grad_mixed_refs[q][...] = grad_mixed[quarter * q : quarter * (q + 1), :]


def token_grads(place, gain, out_proj, returned, normed, inv_std, mixed, cot, earlier):
    tokens, width = normed.shape
    return on_staged(
        token_kernel,
        (place, gain, out_proj, returned, normed, inv_std, *mixed, cot),
        earlier,
        [jax.ShapeDtypeStruct((tokens // 4, width), jnp.bfloat16)] * 8
        + [jax.ShapeDtypeStruct((width, width), jnp.bfloat16)],
        "token_grads",
    )


def share_kernel(shares_ref, *refs):
    total = jnp.sum(shares_ref[...].astype(jnp.float32), axis=0, keepdims=True)
    refs[-1][...] = jnp.broadcast_to(total.astype(jnp.bfloat16), shares_ref.shape)


def pass_kernel(array_ref, *refs):
    refs[-1][...] = array_ref[...]


def after(array, earlier):
    return on_staged(
        pass_kernel, (array,), earlier, jax.ShapeDtypeStruct(array.shape, array.dtype), "after"
    )


def share_sum(shares, earlier):
    return on_staged(
        share_kernel, (shares,), earlier, jax.ShapeDtypeStruct(shares.shape, shares.dtype), "share_sum"
    )


def shards(
    queries,
    key_vectors,
    values,
    residual,
    cotangent,
    out_proj,
    norm_gain,
    router,
    expert_in,
    expert_out,
    expert_id,
    slot_index,
):
    f32, bf16 = jnp.float32, jnp.bfloat16
    side = queries.shape[0]
    width = queries.shape[2]
    head_size = width // HEADS
    tokens = side * side
    quarter = tokens // 4
    expert_count = router.shape[1]
    local_experts = expert_in.shape[0]
    capacity = 2 * tokens // expert_count
    slots_total = expert_count * capacity
    grid_rows, grid_cols = lax.axis_size(GY), lax.axis_size(GX)
    row, col = lax.axis_index(GY), lax.axis_index(GX)
    core = lax.axis_index("c")
    gain = norm_gain[None, :]

    pieces = image_to_window(quarters([queries, key_vectors, values]))

    place = (
        (expert_id * capacity + slot_index)
        .reshape(2, side // 2, 2, side // 2)
        .transpose(0, 2, 1, 3)
        .reshape(1, tokens)
    )
    cot_slots, cot, residual = to_slots(place, cotangent, residual, slots_total, pieces[1:])

    def exchange(slots):
        arrived = lax.all_to_all(slots, GX, 0, 0, tiled=True)
        return (
            arrived.reshape(grid_cols, local_experts, capacity, width)
            .transpose(1, 0, 2, 3)
            .reshape(local_experts, grid_cols * capacity, width)
        )

    slot_cot = exchange(cot_slots)
    cot_pair = lax.all_gather(slot_cot, "yh")

    last = (2 * (row == grid_rows - 1) + (col == grid_cols - 1)).astype(jnp.int32)[None]
    front = attend(last, pieces, quarter, head_size, 0, ())
    back = attend(last, pieces, quarter, head_size, 1, ())
    mixed = window_to_image([jnp.concatenate((front[p], back[p]), axis=1) for p in range(4)])

    slots, normed, inv_std = norm(place, gain, out_proj, mixed, residual, slots_total, ())

    slot_hidden = exchange(slots)
    hidden_pair = lax.all_gather(slot_hidden, "yh")
    router_rows = lax.dynamic_slice_in_dim(router, col * local_experts, local_experts, 1).T.astype(f32)[:, None]
    grad_hidden_slot, small = experts(
        slot_hidden, slot_cot, expert_in, expert_out, router_rows, gain
    )
    returning = (
        grad_hidden_slot.reshape(local_experts, grid_cols, capacity, width)
        .transpose(1, 0, 2, 3)
        .reshape(slots_total, width)
    )
    returned = lax.all_to_all(returning, GX, 0, 0, tiled=True)

    far_in, far_out, upward, downward, own_sums, sums_done = weight_sums(
        hidden_pair, cot_pair, router_rows, expert_in, expert_out, (small,)
    )
    far_in, far_out = step(far_in, 1), step(far_out, -1)
    upward, downward = join(upward, downward, far_in, far_out)
    from_below, from_above = step(upward, 1), step(downward, -1)

    outcome = token_grads(place, gain, out_proj, returned, normed, inv_std, mixed, cot, (sums_done,))
    grad_input, grad_mixed_image, proj_part = outcome[:4], outcome[4:8], outcome[8]
    grad_mixed = image_to_window(grad_mixed_image)

    grads = attend_back(pieces, grad_mixed, (front[4], back[4]), quarter, head_size, ())

    router_table = lax.dynamic_update_slice(
        jnp.zeros((expert_count, width), bf16), small[:, 0].astype(bf16), (col * local_experts, 0)
    )
    gain_row = jnp.sum(small[:, 1], axis=0, keepdims=True).astype(bf16)
    table = jnp.concatenate(
        (proj_part, router_table, jnp.pad(gain_row, ((0, width // 8 - 1), (0, 0)))), axis=0
    )
    table_half = table.shape[0] // 2
    table = table.reshape(2, table_half, width)
    mine = lax.dynamic_index_in_dim(table, core, 0, keepdims=False)
    theirs = lax.dynamic_index_in_dim(table, 1 - core, 0, keepdims=False)
    paired = (mine.astype(f32) + swap(theirs, "c").astype(f32)).astype(bf16)
    peers = GY + ("g",)
    peer_count = lax.axis_size(peers)
    shares = lax.all_to_all(paired.reshape(peer_count, -1, 128), peers, 0, 0, tiled=True)
    summed = lax.all_to_all(share_sum(shares, (grads[0], upward)), peers, 0, 0, tiled=True)
    image_out = tiles(window_to_image(grads), 3, side)
    summed = after(summed, image_out[:1]).reshape(table_half, width)
    sibling = swap(summed, "c")
    full = jnp.where(
        core == 0, jnp.concatenate((summed, sibling), axis=0), jnp.concatenate((sibling, summed), axis=0)
    )
    grad_proj = full[:width]
    grad_router = full[width : width + expert_count].T.astype(f32)
    grad_gain = full[width + expert_count].astype(f32)

    grad_in, grad_out = weight_total(own_sums, from_below, from_above)

    return (
        image_out[0],
        image_out[1],
        image_out[2],
        tiles(grad_input, 1, side)[0],
        grad_proj,
        grad_gain,
        grad_router,
        grad_in,
        grad_out,
    )


def solution(mesh):
    rows, cols = mesh.devices.shape
    split = Mesh(mesh.devices.reshape(2, rows // 2, cols // 2, 2), EVERY)
    tile = P(GY, GX, None)
    return jax.shard_map(
        shards,
        mesh=split,
        in_specs=(tile,) * 5 + (P(), P(), P(), P(GX, None, None), P(GX, None, None), P(GY, GX), P(GY, GX)),
        out_specs=(tile,) * 4 + (P(), P(), P(), P(GX, None, GY), P(GX, GY, None)),
        check_vma=False,
    )
```

```python
import functools

import jax
import jax.numpy as jnp
from jax import lax
from jax.experimental import pallas as pl
from jax.experimental.pallas import tpu as pltpu
from jax.sharding import Mesh
from jax.sharding import PartitionSpec as P

HEADS = 16
EPSILON = 1e-05
NEGATIVE = -1e30
GELU_COEF = 0.7978845608028654
CUBIC_COEF = 0.044715
GY = ("yh", "x")
GX = ("g", "c")
EVERY = GY + GX
ANY = pl.BlockSpec(memory_space=pl.ANY)
VMEM = pl.BlockSpec(memory_space=pltpu.VMEM)
SMEM = pl.BlockSpec(memory_space=pltpu.SMEM)


def fetch(block, down, right):
    rows, cols = lax.axis_size(GY), lax.axis_size(GX)
    if down == 0 and right == 0:
        return block
    if down == 0:
        return lax.ppermute(block, GX, [((j + right) % cols, j) for j in range(cols)])
    if right == 0:
        return lax.ppermute(block, GY, [((i + down) % rows, i) for i in range(rows)])
    route = [
        (((i + down) % rows) * cols + (j + right) % cols, i * cols + j)
        for i in range(rows)
        for j in range(cols)
    ]
    return lax.ppermute(block, EVERY, route)


def swap(block, axis):
    return lax.ppermute(block, axis, [(0, 1), (1, 0)])


def step(block, way):
    size = lax.axis_size("x")
    return lax.ppermute(block, "x", [(i, (i + way) % size) for i in range(size)])


def image_to_window(quarters):
    return [fetch(quarters[3 - p], p // 2, p % 2) for p in range(4)]


def window_to_image(pieces):
    return [fetch(pieces[3 - q], -((3 - q) // 2), -((3 - q) % 2)) for q in range(4)]


def gelu_parts(inputs):
    square = inputs * inputs
    factor = GELU_COEF + (GELU_COEF * CUBIC_COEF) * square
    tangent = jnp.tanh(inputs * factor)
    share = 0.5 + 0.5 * tangent
    value = inputs * share
    slope = share + value * (1.0 - tangent) * (3.0 * factor - 2.0 * GELU_COEF)
    return value, slope

NN = (((1,), (0,)), ((), ()))
NT = (((1,), (1,)), ((), ()))
TN = (((0,), (0,)), ((), ()))
GROUP = 128


def mul(a, b, dims):
    return lax.dot_general(a, b, dims, preferred_element_type=jnp.float32)


def window_parts(pieces, quarter):
    return [
        jnp.concatenate([p[quarter * n : quarter * (n + 1), :] for p in pieces], axis=0) for n in range(3)
    ]


def attend_kernel(quarter, head_size, last_ref, *refs):
    pieces, mixed_refs, probs_ref = refs[:4], refs[-5:-1], refs[-1]
    query, key, value = window_parts(pieces, quarter)
    tokens = query.shape[0]
    of_key = lax.broadcasted_iota(jnp.int32, (tokens, tokens), 0)
    of_query = lax.broadcasted_iota(jnp.int32, (tokens, tokens), 1)
    differs = jnp.bitwise_xor(of_key // quarter, of_query // quarter)
    hidden = jnp.bitwise_and(differs, last_ref[0]) != 0
    scale = head_size ** (-0.5)
    lane_head = lax.broadcasted_iota(jnp.int32, query.shape, 1) // head_size
    value_t = value.T
    mixed_t = []
    for h in range(GROUP // head_size):
        masked = jnp.where(lane_head == h, query, jnp.zeros_like(query))
        scores = mul(key, masked, NT) * scale
        scores = jnp.where(hidden, NEGATIVE, scores)
        weights = jnp.exp(scores - jnp.max(scores, axis=0, keepdims=True))
        probs = (weights * (1.0 / jnp.sum(weights, axis=0, keepdims=True))).astype(jnp.bfloat16)
        probs_ref[h] = probs
        mixed_t.append(mul(value_t[h * head_size : (h + 1) * head_size, :], probs, NN))
    mixed = jnp.concatenate(mixed_t, axis=0).T.astype(jnp.bfloat16)
    for p in range(4):
        mixed_refs[p][...] = mixed[quarter * p : quarter * (p + 1), :]


def attend_back_kernel(quarter, head_size, *refs):
    pieces, grad_refs, probs_refs, outs = refs[:4], refs[4:8], refs[8:10], refs[-4:]
    front = pl.program_id(0) < pl.num_programs(0) // 2
    query, key, value = window_parts(pieces, quarter)
    grad = jnp.concatenate([r[...] for r in grad_refs], axis=0)
    scale = head_size ** (-0.5)
    lane_head = lax.broadcasted_iota(jnp.int32, query.shape, 1) // head_size
    key_t = key.T
    grad_query_t = []
    grad_key = jnp.zeros(query.shape, jnp.float32)
    grad_value = jnp.zeros(query.shape, jnp.float32)
    for h in range(GROUP // head_size):
        mine = lane_head == h
        masked_grad = jnp.where(mine, grad, jnp.zeros_like(grad))
        masked_query = jnp.where(mine, query, jnp.zeros_like(query))
        probs_low = jnp.where(front, probs_refs[0][h], probs_refs[1][h])
        probs = probs_low.astype(jnp.float32)
        grad_probs = mul(value, masked_grad, NT)
        total = jnp.sum(probs * grad_probs, axis=0, keepdims=True)
        grad_scores = (probs * (grad_probs - total) * scale).astype(jnp.bfloat16)
        grad_value += mul(probs_low, masked_grad, NN)
        grad_key += mul(grad_scores, masked_query, NN)
        grad_query_t.append(mul(key_t[h * head_size : (h + 1) * head_size, :], grad_scores, NN))
    grad_query = jnp.concatenate(grad_query_t, axis=0).T
    for n, g in enumerate((grad_query, grad_key, grad_value)):
        low = g.astype(jnp.bfloat16)
        for p in range(4):
            outs[p][quarter * n : quarter * (n + 1), :] = low[quarter * p : quarter * (p + 1), :]


def staged(kernel, count, *refs):
    inputs, (buffers, sems) = refs[:count], (refs[-1 - count : -1], refs[-1])
    copies = [pltpu.make_async_copy(inputs[n], buffers[n], sems.at[n]) for n in range(count)]
    for copy in copies:
        copy.start()
    for copy in copies:
        copy.wait()
    kernel(*buffers, *refs[count : -1 - count])


def on_staged(kernel, inputs, earlier, out_shape, name, flops=0):
    return pl.pallas_call(
        functools.partial(staged, kernel, len(inputs)),
        in_specs=[ANY] * (len(inputs) + len(earlier)),
        out_shape=out_shape,
        scratch_shapes=[pltpu.VMEM(x.shape, x.dtype) for x in inputs]
        + [pltpu.SemaphoreType.DMA((len(inputs),))],
        compiler_params=params(),
        cost_estimate=pl.CostEstimate(flops=flops, bytes_accessed=1, transcendentals=0),
        name=name,
    )(*inputs, *earlier)


def params():
    return pltpu.CompilerParams(vmem_limit_bytes=60 * 1024 * 1024)


def attend(last, pieces, quarter, head_size, part, earlier):
    tokens, width = 4 * quarter, pieces[0].shape[1] // 2
    heads, groups = GROUP // head_size, width // GROUP
    return pl.pallas_call(
        functools.partial(attend_kernel, quarter, head_size),
        grid=(groups,),
        in_specs=[SMEM]
        + [pl.BlockSpec((3 * quarter, GROUP), lambda g: (0, g + part * groups))] * 4
        + [ANY] * len(earlier),
        out_specs=[pl.BlockSpec((quarter, GROUP), lambda g: (0, g))] * 4
        + [pl.BlockSpec((heads, tokens, tokens), lambda g: (g, 0, 0))],
        out_shape=[jax.ShapeDtypeStruct((quarter, width), jnp.bfloat16)] * 4
        + [jax.ShapeDtypeStruct((width // head_size, tokens, tokens), jnp.bfloat16)],
        compiler_params=params(),
        cost_estimate=pl.CostEstimate(
            flops=16 * tokens * tokens * width, bytes_accessed=12 * tokens * width, transcendentals=0
        ),
        name="attend",
    )(last, *pieces, *earlier)


def attend_back(pieces, grads, probs, quarter, head_size, earlier):
    tokens, width = 4 * quarter, pieces[0].shape[1]
    heads, groups = GROUP // head_size, width // GROUP
    return pl.pallas_call(
        functools.partial(attend_back_kernel, quarter, head_size),
        grid=(groups,),
        in_specs=[pl.BlockSpec((3 * quarter, GROUP), lambda g: (0, g))] * 4
        + [pl.BlockSpec((quarter, GROUP), lambda g: (0, g))] * 4
        + [
            pl.BlockSpec((heads, tokens, tokens), lambda g: (jnp.minimum(g, groups // 2 - 1), 0, 0)),
            pl.BlockSpec((heads, tokens, tokens), lambda g: (jnp.maximum(g - groups // 2, 0), 0, 0)),
        ]
        + [ANY] * len(earlier),
        out_specs=[pl.BlockSpec((3 * quarter, GROUP), lambda g: (0, g))] * 4,
        out_shape=[jax.ShapeDtypeStruct((3 * quarter, width), jnp.bfloat16)] * 4,
        compiler_params=params(),
        cost_estimate=pl.CostEstimate(
            flops=8 * tokens * tokens * width * 4, bytes_accessed=12 * tokens * width * 2, transcendentals=0
        ),
        name="attend_back",
    )(*pieces, *grads, *probs, *earlier)


def bring(sources, buffers, sems):
    copies = [pltpu.make_async_copy(s, b, sems.at[n]) for n, (s, b) in enumerate(zip(sources, buffers))]
    for copy in copies:
        copy.start()
    return copies


def expert_kernel(chunk, hidden_hbm, cot_hbm, router_hbm, gain_hbm, in_hbm, out_hbm, *refs):
    back_ref, small_ref, ins, outs, sems, hidden_ref, cot_ref, router_ref, gain_ref, few_sems = refs[-10:]
    f32 = jnp.float32
    count, chunks = ins.shape[:2]
    few = bring(
        (hidden_hbm, router_hbm, cot_hbm, gain_hbm), (hidden_ref, router_ref, cot_ref, gain_ref), few_sems
    )
    copies = {}
    for e in range(count):
        for c in range(chunks):
            units = pl.ds(chunk * c, chunk)
            copies[e, c] = (
                pltpu.make_async_copy(in_hbm.at[e, :, units], ins.at[e, c], sems.at[0, e, c]),
                pltpu.make_async_copy(out_hbm.at[e, units, :], outs.at[e, c], sems.at[1, e, c]),
            )
            for copy in copies[e, c]:
                copy.start()
    for copy in few:
        copy.wait()
    for e in range(count):
        slots = hidden_ref[e]
        wide = slots.astype(f32)
        router_row = router_ref[e]
        logit = jnp.sum(wide * router_row, axis=-1, keepdims=True)
        gate = 1.0 / (1.0 + jnp.exp(-logit))
        gate_low = gate.astype(jnp.bfloat16).astype(f32)
        total, gate_sum = 0.0, 0.0
        for c in range(chunks):
            for copy in copies[e, c]:
                copy.wait()
            weight, spread = ins[e, c], mul(cot_ref[e], outs[e, c], NT)
            activated, slope = gelu_parts(mul(slots, weight, NN))
            gate_sum += jnp.sum(activated * spread, axis=-1, keepdims=True)
            total += mul((gate_low * spread * slope).astype(jnp.bfloat16), weight, NT)
        grad_logit = gate_sum * gate * (1.0 - gate)
        grad_hidden = total + grad_logit * router_row
        back_ref[e] = grad_hidden.astype(jnp.bfloat16)
        small_ref[e, 0:1, :] = jnp.sum(wide * grad_logit, axis=0, keepdims=True)
        small_ref[e, 1:2, :] = jnp.sum(wide * grad_hidden, axis=0, keepdims=True) / gain_ref[...]


def experts(slot_hidden, slot_cot, expert_in, expert_out, router_rows, gain, earlier):
    count, slots, width = slot_hidden.shape
    hidden = expert_in.shape[2]
    chunk = min(hidden, 512)
    chunks = hidden // chunk
    return pl.pallas_call(
        functools.partial(expert_kernel, chunk),
        in_specs=[ANY] * (6 + len(earlier)),
        out_shape=[
            jax.ShapeDtypeStruct((count, slots, width), jnp.bfloat16),
            jax.ShapeDtypeStruct((count, 2, width), jnp.float32),
        ],
        scratch_shapes=[
            pltpu.VMEM((count, chunks, width, chunk), jnp.bfloat16),
            pltpu.VMEM((count, chunks, chunk, width), jnp.bfloat16),
            pltpu.SemaphoreType.DMA((2, count, chunks)),
            pltpu.VMEM(slot_hidden.shape, slot_hidden.dtype),
            pltpu.VMEM(slot_cot.shape, slot_cot.dtype),
            pltpu.VMEM(router_rows.shape, router_rows.dtype),
            pltpu.VMEM(gain.shape, gain.dtype),
            pltpu.SemaphoreType.DMA((4,)),
        ],
        compiler_params=params(),
        cost_estimate=pl.CostEstimate(
            flops=12 * count * slots * width * hidden, bytes_accessed=8 * count * slots * hidden, transcendentals=0
        ),
        name="experts",
    )(slot_hidden, slot_cot, router_rows, gain, expert_in, expert_out, *earlier)


def weights_kernel(units_ref, *refs):
    f32, bf16 = jnp.float32, jnp.bfloat16
    in_hbm, out_hbm = refs[5:7]
    far_in_ref, far_out_ref, up_ref, down_ref, own_ref, token_ref, ins, outs, sems = refs[-15:-6]
    hidden_refs, cot_refs, router_ref = refs[-6:-4], refs[-4:-2], refs[-2]
    few = bring(refs[:5], refs[-6:-1], refs[-1])
    count, ways, width, part = ins.shape
    copies = {}
    for e in range(count):
        for d in range(ways):
            units = pl.ds(pl.multiple_of(units_ref[d] * part, part), part)
            copies[e, d] = (
                pltpu.make_async_copy(in_hbm.at[e, :, units], ins.at[e, d], sems.at[0, e, d]),
                pltpu.make_async_copy(out_hbm.at[e, units, :], outs.at[e, d], sems.at[1, e, d]),
            )
            for copy in copies[e, d]:
                copy.start()
    token_ref[...] = jnp.zeros_like(token_ref)
    for copy in few:
        copy.wait()
    for e in range(count):
        slots = jnp.concatenate([r[e] for r in hidden_refs], axis=0)
        cot = jnp.concatenate([r[e] for r in cot_refs], axis=0)
        logit = jnp.sum(slots.astype(f32) * router_ref[e], axis=-1, keepdims=True)
        gate = (1.0 / (1.0 + jnp.exp(-logit))).astype(bf16).astype(f32)
        scaled = (gate * cot.astype(f32)).astype(bf16)
        slots_t, scaled_t = slots.T, scaled.T
        for d in range(ways):
            for copy in copies[e, d]:
                copy.wait()
            activated, slope = gelu_parts(mul(slots, ins[e, d], NN))
            grad_pre = (mul(scaled, outs[e, d], NT) * slope).astype(bf16)
            sum_in = mul(slots_t, grad_pre, NN)
            sum_out = mul(scaled_t, activated.astype(bf16), NN)
            if d == 0:
                far_in_ref[e] = sum_in.astype(bf16)
                far_out_ref[e] = sum_out.astype(bf16)
            else:
                target = (up_ref, down_ref, own_ref)[d - 1]
                target[0, e] = sum_in.astype(target.dtype)
                target[1, e] = sum_out.astype(target.dtype)


def weight_sums(hidden_rows, cot_rows, router_rows, expert_in, expert_out, earlier):
    count, slots, width = hidden_rows[0].shape
    along = lax.axis_size("x")
    part = expert_in.shape[2] // (2 * along)
    half, place = lax.axis_index("yh"), lax.axis_index("x")
    units = jnp.stack([half * along + (place + way) % along for way in (2, 1, -1, 0)]).astype(jnp.int32)
    bf16, f32 = jnp.bfloat16, jnp.float32
    return pl.pallas_call(
        weights_kernel,
        in_specs=[SMEM] + [ANY] * (7 + len(earlier)),
        out_shape=[jax.ShapeDtypeStruct((count, width, part), bf16)] * 2
        + [jax.ShapeDtypeStruct((2, count, width, part), t) for t in (bf16, bf16, f32)]
        + [jax.ShapeDtypeStruct((8, 128), f32)],
        scratch_shapes=[
            pltpu.VMEM((count, 4, width, part), bf16),
            pltpu.VMEM((count, 4, part, width), bf16),
            pltpu.SemaphoreType.DMA((2, count, 4)),
        ]
        + [pltpu.VMEM((count, slots, width), bf16)] * 4
        + [pltpu.VMEM(router_rows.shape, f32), pltpu.SemaphoreType.DMA((5,))],
        compiler_params=params(),
        cost_estimate=pl.CostEstimate(
            flops=128 * count * slots * width * part, bytes_accessed=16 * count * slots * width, transcendentals=0
        ),
        name="weight_sums",
    )(units, *hidden_rows, *cot_rows, router_rows, expert_in, expert_out, *earlier)


def join_kernel(up_ref, down_ref, far_in_ref, far_out_ref, up_out, down_out):
    f32, bf16 = jnp.float32, jnp.bfloat16
    up_out[0] = (up_ref[0].astype(f32) + far_in_ref[...].astype(f32)).astype(bf16)
    up_out[1] = up_ref[1]
    down_out[0] = down_ref[0]
    down_out[1] = (down_ref[1].astype(f32) + far_out_ref[...].astype(f32)).astype(bf16)


def join(up, down, far_in, far_out):
    return on_staged(
        join_kernel,
        (up, down, far_in, far_out),
        (),
        [jax.ShapeDtypeStruct(up.shape, up.dtype)] * 2,
        "join",
    )


def weight_total_kernel(own_ref, up_ref, down_ref, grad_in_ref, grad_out_ref):
    f32 = jnp.float32
    total = own_ref[:, 0] + up_ref[:, 0].astype(f32) + down_ref[:, 0].astype(f32)
    grad_in_ref[0] = total[0].astype(jnp.bfloat16)
    grad_out_ref[0] = total[1].T.astype(jnp.bfloat16)


def weight_total(own, up, down):
    _, count, width, part = own.shape
    arrived = pl.BlockSpec((2, 1, width, part), lambda e: (0, e, 0, 0))
    return pl.pallas_call(
        weight_total_kernel,
        grid=(count,),
        in_specs=[arrived] * 3,
        out_specs=[
            pl.BlockSpec((1, width, part), lambda e: (e, 0, 0)),
            pl.BlockSpec((1, part, width), lambda e: (e, 0, 0)),
        ],
        out_shape=[
            jax.ShapeDtypeStruct((count, width, part), jnp.bfloat16),
            jax.ShapeDtypeStruct((count, part, width), jnp.bfloat16),
        ],
        compiler_params=params(),
        name="weight_total",
    )(own, up, down)


def quarter_of(tile_ref, q):
    half = tile_ref.shape[0] // 2
    a, b = q // 2, q % 2
    block = tile_ref[half * a : half * (a + 1), half * b : half * (b + 1), :]
    return block.reshape(half * half, tile_ref.shape[2])


def quarters_kernel(count, *refs):
    outs, (buffer, sems) = refs[count : count + 4], refs[-2:]
    copies = [pltpu.make_async_copy(refs[n], buffer.at[n], sems.at[n]) for n in range(count)]
    for copy in copies:
        copy.start()
    for n in range(count):
        copies[n].wait()
        for q in range(4):
            block = quarter_of(buffer.at[n], q)
            rows = block.shape[0]
            outs[q][rows * n : rows * (n + 1), :] = block


def quarters(tiles):
    side, _, width = tiles[0].shape
    count = len(tiles)
    return pl.pallas_call(
        functools.partial(quarters_kernel, count),
        in_specs=[ANY] * count,
        out_shape=[jax.ShapeDtypeStruct((count * side * side // 4, width), tiles[0].dtype)] * 4,
        scratch_shapes=[
            pltpu.VMEM((count, side, side, width), tiles[0].dtype),
            pltpu.SemaphoreType.DMA((count,)),
        ],
        compiler_params=params(),
        name="quarters",
    )(*tiles)


def tiles_kernel(count, *refs):
    for n in range(count):
        tile_ref = refs[4 + n]
        half, width = tile_ref.shape[0] // 2, tile_ref.shape[2]
        for q in range(4):
            a, b = q // 2, q % 2
            block = refs[q][half * half * n : half * half * (n + 1), :].reshape(half, half, width)
            tile_ref[half * a : half * (a + 1), half * b : half * (b + 1), :] = block


def tiles(parts, count, side):
    width = parts[0].shape[1]
    return pl.pallas_call(
        functools.partial(tiles_kernel, count),
        grid=(width // GROUP,),
        in_specs=[pl.BlockSpec((parts[0].shape[0], GROUP), lambda g: (0, g))] * 4,
        out_specs=[pl.BlockSpec((side, side, GROUP), lambda g: (0, 0, g))] * count,
        out_shape=[jax.ShapeDtypeStruct((side, side, width), parts[0].dtype)] * count,
        compiler_params=params(),
        name="tiles",
    )(*parts)


def slot_picker(place_ref, slots):
    place = place_ref[...]
    index = lax.broadcasted_iota(jnp.int32, (slots, place.shape[1]), 0)
    return (index == place).astype(jnp.bfloat16)


def to_slots_kernel(place_ref, cot_hbm, residual_hbm, *refs):
    slots_ref, cot_ref, residual_ref, buffer, sems = refs[-5:]
    copies = [
        pltpu.make_async_copy(hbm, buffer.at[n], sems.at[n]) for n, hbm in enumerate((cot_hbm, residual_hbm))
    ]
    for copy in copies:
        copy.start()
    for n, out in enumerate((cot_ref, residual_ref)):
        copies[n].wait()
        for q in range(4):
            block = quarter_of(buffer.at[n], q)
            rows = block.shape[0]
            out[rows * q : rows * (q + 1), :] = block
        if n == 0:
            picker = slot_picker(place_ref, slots_ref.shape[0])
            slots_ref[...] = mul(picker, cot_ref[...], NN).astype(slots_ref.dtype)


def to_slots(place, cotangent, residual, slots, earlier):
    side, _, width = cotangent.shape
    low = cotangent.dtype
    return pl.pallas_call(
        to_slots_kernel,
        in_specs=[VMEM, ANY, ANY] + [ANY] * len(earlier),
        out_shape=[jax.ShapeDtypeStruct((slots, width), low)]
        + [jax.ShapeDtypeStruct((side * side, width), low)] * 2,
        scratch_shapes=[pltpu.VMEM((2, side, side, width), low), pltpu.SemaphoreType.DMA((2,))],
        compiler_params=params(),
        name="to_slots",
    )(place, cotangent, residual, *earlier)


def norm_kernel(place_ref, gain_ref, proj_ref, *refs):
    f32, bf16 = jnp.float32, jnp.bfloat16
    mixed_refs = refs[:4]
    residual_ref, slots_ref, normed_ref, inv_ref = refs[4], *refs[-3:]
    mixed = jnp.concatenate([r[...] for r in mixed_refs], axis=0)
    attended = mul(mixed, proj_ref[...], NN).astype(bf16)
    stream = residual_ref[...].astype(f32) + attended.astype(f32)
    centered = stream - jnp.mean(stream, axis=-1, keepdims=True)
    inv_std = lax.rsqrt(jnp.mean(centered * centered, axis=-1, keepdims=True) + EPSILON)
    normed = centered * inv_std
    hidden_in = (normed * gain_ref[...]).astype(bf16)
    normed_ref[...] = normed
    inv_ref[...] = inv_std
    slots_ref[...] = mul(slot_picker(place_ref, slots_ref.shape[0]), hidden_in, NN).astype(bf16)


def norm(place, gain, out_proj, mixed, residual, slots, earlier):
    tokens, width = place.shape[1], out_proj.shape[0]
    return on_staged(
        norm_kernel,
        (place, gain, out_proj, *mixed, residual),
        earlier,
        [
            jax.ShapeDtypeStruct((slots, width), jnp.bfloat16),
            jax.ShapeDtypeStruct((tokens, width), jnp.float32),
            jax.ShapeDtypeStruct((tokens, 1), jnp.float32),
        ],
        "norm",
    )


def token_kernel(place_ref, gain_ref, proj_ref, returned_ref, normed_ref, inv_ref, *refs):
    f32, bf16 = jnp.float32, jnp.bfloat16
    mixed_refs, cot_ref = refs[:4], refs[4]
    grad_refs, grad_mixed_refs, part_ref = refs[-9:-5], refs[-5:-1], refs[-1]
    mixed = jnp.concatenate([r[...] for r in mixed_refs], axis=0)
    cot = cot_ref[...]
    normed, inv_std = normed_ref[...], inv_ref[...]
    grad_hidden = mul(slot_picker(place_ref, returned_ref.shape[0]), returned_ref[...], TN)
    grad = grad_hidden * gain_ref[...]
    grad_input = (
        cot.astype(f32)
        + inv_std
        * (
            grad
            - jnp.mean(grad, axis=-1, keepdims=True)
            - normed * jnp.mean(grad * normed, axis=-1, keepdims=True)
        )
    ).astype(bf16)
    grad_mixed = mul(grad_input, proj_ref[...], NT).astype(bf16)
    part_ref[...] = mul(mixed, grad_input, TN).astype(bf16)
    quarter = grad_refs[0].shape[0]
    for q in range(4):
        grad_refs[q][...] = grad_input[quarter * q : quarter * (q + 1), :]
        grad_mixed_refs[q][...] = grad_mixed[quarter * q : quarter * (q + 1), :]


def token_grads(place, gain, out_proj, returned, normed, inv_std, mixed, cot, earlier):
    tokens, width = normed.shape
    return on_staged(
        token_kernel,
        (place, gain, out_proj, returned, normed, inv_std, *mixed, cot),
        earlier,
        [jax.ShapeDtypeStruct((tokens // 4, width), jnp.bfloat16)] * 8
        + [jax.ShapeDtypeStruct((width, width), jnp.bfloat16)],
        "token_grads",
    )


def to_devices_kernel(rows_ref, *refs):
    out_ref = refs[-1]
    devices, rows, width = out_ref.shape
    count = rows_ref.shape[0]
    parts = [
        rows_ref[e].astype(jnp.float32).reshape(devices, rows // count, width) for e in range(count)
    ]
    out_ref[...] = jnp.concatenate(parts, axis=1).astype(out_ref.dtype)


def to_devices(rows, devices, earlier):
    count, slots, width = rows.shape
    shape = jax.ShapeDtypeStruct((devices, count * slots // devices, width), rows.dtype)
    return on_staged(to_devices_kernel, (rows,), earlier, shape, "to_devices")


def pass_kernel(array_ref, *refs):
    refs[-1][...] = array_ref[...]


def after(array, earlier):
    shape = jax.ShapeDtypeStruct(array.shape, array.dtype)
    return on_staged(pass_kernel, (array,), earlier, shape, "after")


def share_kernel(further, shares_ref, *refs):
    total = jnp.sum(shares_ref[...].astype(jnp.float32), axis=0)
    out_ref = refs[-1]
    total = jnp.concatenate([total] + [r[...] for r in refs[:further]], axis=0).astype(jnp.bfloat16)
    out_ref[...] = jnp.broadcast_to(total[None], out_ref.shape)


def share_sum(inputs, copies, earlier):
    rows = inputs[0].shape[1] + sum(x.shape[0] for x in inputs[1:])
    shape = jax.ShapeDtypeStruct((copies, rows, inputs[0].shape[2]), inputs[0].dtype)
    kernel = functools.partial(share_kernel, len(inputs) - 1)
    return on_staged(kernel, inputs, earlier, shape, "share_sum")


def shards(
    queries,
    key_vectors,
    values,
    residual,
    cotangent,
    out_proj,
    norm_gain,
    router,
    expert_in,
    expert_out,
    expert_id,
    slot_index,
):
    f32, bf16 = jnp.float32, jnp.bfloat16
    side = queries.shape[0]
    width = queries.shape[2]
    head_size = width // HEADS
    tokens = side * side
    quarter = tokens // 4
    expert_count = router.shape[1]
    local_experts = expert_in.shape[0]
    capacity = 2 * tokens // expert_count
    slots_total = expert_count * capacity
    grid_rows, grid_cols = lax.axis_size(GY), lax.axis_size(GX)
    row, col = lax.axis_index(GY), lax.axis_index(GX)
    core = lax.axis_index("c")
    gain = norm_gain[None, :]

    pieces = image_to_window(quarters([queries, key_vectors, values]))

    place = (
        (expert_id * capacity + slot_index)
        .reshape(2, side // 2, 2, side // 2)
        .transpose(0, 2, 1, 3)
        .reshape(1, tokens)
    )
    cot_slots, cot, residual = to_slots(place, cotangent, residual, slots_total, pieces[1:])

    def exchange(slots):
        arrived = lax.all_to_all(slots, GX, 0, 0, tiled=True)
        return (
            arrived.reshape(grid_cols, local_experts, capacity, width)
            .transpose(1, 0, 2, 3)
            .reshape(local_experts, grid_cols * capacity, width)
        )

    slot_cot = exchange(cot_slots)
    other_cot = swap(slot_cot, "yh")

    last = (2 * (row == grid_rows - 1) + (col == grid_cols - 1)).astype(jnp.int32)[None]
    front = attend(last, pieces, quarter, head_size, 0, ())
    back = attend(last, pieces, quarter, head_size, 1, ())
    mixed = window_to_image([jnp.concatenate((front[p], back[p]), axis=1) for p in range(4)])

    slots, normed, inv_std = norm(place, gain, out_proj, mixed, residual, slots_total, ())

    slot_hidden = exchange(slots)
    other_hidden = swap(slot_hidden, "yh")
    router_rows = lax.dynamic_slice_in_dim(router, col * local_experts, local_experts, 1).T.astype(f32)[:, None]
    grad_hidden_slot, small = experts(
        slot_hidden, slot_cot, expert_in, expert_out, router_rows, gain, (other_cot,)
    )
    returning = to_devices(grad_hidden_slot, grid_cols, (other_hidden,))
    returned = lax.all_to_all(returning, GX, 0, 0, tiled=True).reshape(slots_total, width)

    far_in, far_out, upward, downward, own_sums, sums_done = weight_sums(
        (slot_hidden, other_hidden),
        (slot_cot, other_cot),
        router_rows,
        expert_in,
        expert_out,
        (small,),
    )
    far_in, far_out = step(far_in, 1), step(far_out, -1)
    upward, downward = join(upward, downward, far_in, far_out)
    from_below, from_above = step(upward, 1), step(downward, -1)

    outcome = token_grads(place, gain, out_proj, returned, normed, inv_std, mixed, cot, (sums_done,))
    grad_input, grad_mixed_image, proj_part = outcome[:4], outcome[4:8], outcome[8]
    grad_mixed = image_to_window(grad_mixed_image)

    grads = attend_back(pieces, grad_mixed, (front[4], back[4]), quarter, head_size, ())

    extra = jnp.concatenate((small[:, 0], jnp.sum(small[:, 1], axis=0, keepdims=True)), axis=0)
    extra = jnp.pad(extra, ((0, -extra.shape[0] % 8), (0, 0)))
    shares = lax.all_to_all(proj_part.reshape(grid_cols, -1, width), GX, 0, 0, tiled=True)
    shares = lax.all_to_all(share_sum((shares, extra), grid_rows, (grads[0],)), GY, 0, 0, tiled=True)
    summed = lax.all_to_all(share_sum((shares,), grid_cols, (upward,)), GX, 0, 0, tiled=True)
    image_out = tiles(window_to_image(grads), 3, side)
    summed = after(summed, image_out[:1])
    proj_rows = width // grid_cols
    grad_proj = summed[:, :proj_rows].reshape(width, width)
    grad_router = summed[:, proj_rows : proj_rows + local_experts].reshape(expert_count, width).T.astype(f32)
    grad_gain = jnp.sum(summed[:, proj_rows + local_experts].astype(f32), axis=0)
    grad_in, grad_out = weight_total(own_sums, from_below, from_above)

    return (
        image_out[0],
        image_out[1],
        image_out[2],
        tiles(grad_input, 1, side)[0],
        grad_proj,
        grad_gain,
        grad_router,
        grad_in,
        grad_out,
    )


def solution(mesh):
    rows, cols = mesh.devices.shape
    split = Mesh(mesh.devices.reshape(2, rows // 2, cols // 2, 2), EVERY)
    tile = P(GY, GX, None)
    return jax.shard_map(
        shards,
        mesh=split,
        in_specs=(tile,) * 5 + (P(), P(), P(), P(GX, None, None), P(GX, None, None), P(GY, GX), P(GY, GX)),
        out_specs=(tile,) * 4 + (P(), P(), P(), P(GX, None, GY), P(GX, GY, None)),
        check_vma=False,
    )
```

```python
import functools

import jax
import jax.numpy as jnp
from jax import lax
from jax.experimental import pallas as pl
from jax.experimental.pallas import tpu as pltpu
from jax.sharding import Mesh
from jax.sharding import PartitionSpec as P

HEADS = 16
EPSILON = 1e-05
NEGATIVE = -1e30
GELU_COEF = 0.7978845608028654
CUBIC_COEF = 0.044715
GY = ("yh", "x")
GX = ("g", "c")
EVERY = GY + GX
ANY = pl.BlockSpec(memory_space=pl.ANY)
VMEM = pl.BlockSpec(memory_space=pltpu.VMEM)
SMEM = pl.BlockSpec(memory_space=pltpu.SMEM)


def fetch(block, down, right):
    rows, cols = lax.axis_size(GY), lax.axis_size(GX)
    if down == 0 and right == 0:
        return block
    if down == 0:
        return lax.ppermute(block, GX, [((j + right) % cols, j) for j in range(cols)])
    if right == 0:
        return lax.ppermute(block, GY, [((i + down) % rows, i) for i in range(rows)])
    route = [
        (((i + down) % rows) * cols + (j + right) % cols, i * cols + j)
        for i in range(rows)
        for j in range(cols)
    ]
    return lax.ppermute(block, EVERY, route)


def swap(block, axis):
    return lax.ppermute(block, axis, [(0, 1), (1, 0)])


def step(block, way):
    size = lax.axis_size("x")
    return lax.ppermute(block, "x", [(i, (i + way) % size) for i in range(size)])


def image_to_window(quarters):
    return [fetch(quarters[3 - p], p // 2, p % 2) for p in range(4)]


def window_to_image(pieces):
    return [fetch(pieces[3 - q], -((3 - q) // 2), -((3 - q) % 2)) for q in range(4)]


def gelu_parts(inputs):
    square = inputs * inputs
    factor = GELU_COEF + (GELU_COEF * CUBIC_COEF) * square
    tangent = jnp.tanh(inputs * factor)
    share = 0.5 + 0.5 * tangent
    value = inputs * share
    slope = share + value * (1.0 - tangent) * (3.0 * factor - 2.0 * GELU_COEF)
    return value, slope

NN = (((1,), (0,)), ((), ()))
NT = (((1,), (1,)), ((), ()))
TN = (((0,), (0,)), ((), ()))
GROUP = 128


def mul(a, b, dims):
    return lax.dot_general(a, b, dims, preferred_element_type=jnp.float32)


def window_parts(pieces, quarter):
    return [
        jnp.concatenate([p[quarter * n : quarter * (n + 1), :] for p in pieces], axis=0) for n in range(3)
    ]


def attend_kernel(quarter, head_size, last_ref, *refs):
    pieces, mixed_refs, probs_ref = refs[:4], refs[-5:-1], refs[-1]
    query, key, value = window_parts(pieces, quarter)
    tokens = query.shape[0]
    of_key = lax.broadcasted_iota(jnp.int32, (tokens, tokens), 0)
    of_query = lax.broadcasted_iota(jnp.int32, (tokens, tokens), 1)
    differs = jnp.bitwise_xor(of_key // quarter, of_query // quarter)
    hidden = jnp.bitwise_and(differs, last_ref[0]) != 0
    scale = head_size ** (-0.5)
    lane_head = lax.broadcasted_iota(jnp.int32, query.shape, 1) // head_size
    value_t = value.T
    mixed_t = []
    for h in range(GROUP // head_size):
        masked = jnp.where(lane_head == h, query, jnp.zeros_like(query))
        scores = mul(key, masked, NT) * scale
        scores = jnp.where(hidden, NEGATIVE, scores)
        weights = jnp.exp(scores - jnp.max(scores, axis=0, keepdims=True))
        probs = (weights * (1.0 / jnp.sum(weights, axis=0, keepdims=True))).astype(jnp.bfloat16)
        probs_ref[h] = probs
        mixed_t.append(mul(value_t[h * head_size : (h + 1) * head_size, :], probs, NN))
    mixed = jnp.concatenate(mixed_t, axis=0).T.astype(jnp.bfloat16)
    for p in range(4):
        mixed_refs[p][...] = mixed[quarter * p : quarter * (p + 1), :]


def attend_back_kernel(quarter, head_size, *refs):
    pieces, grad_refs, probs_ref, outs = refs[:4], refs[4:8], refs[8], refs[-4:]
    query, key, value = window_parts(pieces, quarter)
    grad = jnp.concatenate([r[...] for r in grad_refs], axis=0)
    scale = head_size ** (-0.5)
    lane_head = lax.broadcasted_iota(jnp.int32, query.shape, 1) // head_size
    key_t = key.T
    grad_query_t = []
    grad_key = jnp.zeros(query.shape, jnp.float32)
    grad_value = jnp.zeros(query.shape, jnp.float32)
    for h in range(GROUP // head_size):
        mine = lane_head == h
        masked_grad = jnp.where(mine, grad, jnp.zeros_like(grad))
        masked_query = jnp.where(mine, query, jnp.zeros_like(query))
        probs_low = probs_ref[h]
        probs = probs_low.astype(jnp.float32)
        grad_probs = mul(value, masked_grad, NT)
        total = jnp.sum(probs * grad_probs, axis=0, keepdims=True)
        grad_scores = (probs * (grad_probs - total) * scale).astype(jnp.bfloat16)
        grad_value += mul(probs_low, masked_grad, NN)
        grad_key += mul(grad_scores, masked_query, NN)
        grad_query_t.append(mul(key_t[h * head_size : (h + 1) * head_size, :], grad_scores, NN))
    grad_query = jnp.concatenate(grad_query_t, axis=0).T
    for n, g in enumerate((grad_query, grad_key, grad_value)):
        low = g.astype(jnp.bfloat16)
        for p in range(4):
            outs[p][quarter * n : quarter * (n + 1), :] = low[quarter * p : quarter * (p + 1), :]


def staged(kernel, count, *refs):
    inputs, (buffers, sems) = refs[:count], (refs[-1 - count : -1], refs[-1])
    copies = [pltpu.make_async_copy(inputs[n], buffers[n], sems.at[n]) for n in range(count)]
    for copy in copies:
        copy.start()
    for copy in copies:
        copy.wait()
    kernel(*buffers, *refs[count : -1 - count])


def on_staged(kernel, inputs, earlier, out_shape, name, flops=0):
    return pl.pallas_call(
        functools.partial(staged, kernel, len(inputs)),
        in_specs=[ANY] * (len(inputs) + len(earlier)),
        out_shape=out_shape,
        scratch_shapes=[pltpu.VMEM(x.shape, x.dtype) for x in inputs]
        + [pltpu.SemaphoreType.DMA((len(inputs),))],
        compiler_params=params(),
        cost_estimate=pl.CostEstimate(flops=flops, bytes_accessed=1, transcendentals=0),
        name=name,
    )(*inputs, *earlier)


def params():
    return pltpu.CompilerParams(vmem_limit_bytes=60 * 1024 * 1024)


def attend(last, pieces, quarter, head_size):
    tokens, width = 4 * quarter, pieces[0].shape[1]
    heads, groups = GROUP // head_size, width // GROUP
    return pl.pallas_call(
        functools.partial(attend_kernel, quarter, head_size),
        grid=(groups,),
        in_specs=[SMEM]
        + [pl.BlockSpec((3 * quarter, GROUP), lambda g: (0, g))] * 4,
        out_specs=[pl.BlockSpec((quarter, GROUP), lambda g: (0, g))] * 4
        + [pl.BlockSpec((heads, tokens, tokens), lambda g: (g, 0, 0))],
        out_shape=[jax.ShapeDtypeStruct((quarter, width), jnp.bfloat16)] * 4
        + [jax.ShapeDtypeStruct((width // head_size, tokens, tokens), jnp.bfloat16)],
        compiler_params=params(),
        cost_estimate=pl.CostEstimate(
            flops=16 * tokens * tokens * width, bytes_accessed=12 * tokens * width, transcendentals=0
        ),
        name="attend",
    )(last, *pieces)


def attend_back(pieces, grads, probs, quarter, head_size, earlier):
    tokens, width = 4 * quarter, pieces[0].shape[1]
    heads, groups = GROUP // head_size, width // GROUP
    return pl.pallas_call(
        functools.partial(attend_back_kernel, quarter, head_size),
        grid=(groups,),
        in_specs=[pl.BlockSpec((3 * quarter, GROUP), lambda g: (0, g))] * 4
        + [pl.BlockSpec((quarter, GROUP), lambda g: (0, g))] * 4
        + [pl.BlockSpec((heads, tokens, tokens), lambda g: (g, 0, 0))]
        + [ANY] * len(earlier),
        out_specs=[pl.BlockSpec((3 * quarter, GROUP), lambda g: (0, g))] * 4,
        out_shape=[jax.ShapeDtypeStruct((3 * quarter, width), jnp.bfloat16)] * 4,
        compiler_params=params(),
        cost_estimate=pl.CostEstimate(
            flops=8 * tokens * tokens * width * 4, bytes_accessed=12 * tokens * width * 2, transcendentals=0
        ),
        name="attend_back",
    )(*pieces, *grads, probs, *earlier)


def bring(sources, buffers, sems):
    copies = [pltpu.make_async_copy(s, b, sems.at[n]) for n, (s, b) in enumerate(zip(sources, buffers))]
    for copy in copies:
        copy.start()
    return copies


def expert_kernel(chunk, hidden_hbm, cot_hbm, router_hbm, gain_hbm, in_hbm, out_hbm, *refs):
    back_ref, small_ref, ins, outs, sems, hidden_ref, cot_ref, router_ref, gain_ref, few_sems = refs[-10:]
    f32 = jnp.float32
    count, chunks = ins.shape[:2]
    few = bring(
        (hidden_hbm, router_hbm, cot_hbm, gain_hbm), (hidden_ref, router_ref, cot_ref, gain_ref), few_sems
    )
    copies = {}
    for e in range(count):
        for c in range(chunks):
            units = pl.ds(chunk * c, chunk)
            copies[e, c] = (
                pltpu.make_async_copy(in_hbm.at[e, :, units], ins.at[e, c], sems.at[0, e, c]),
                pltpu.make_async_copy(out_hbm.at[e, units, :], outs.at[e, c], sems.at[1, e, c]),
            )
            for copy in copies[e, c]:
                copy.start()
    for copy in few:
        copy.wait()
    for e in range(count):
        slots = hidden_ref[e]
        wide = slots.astype(f32)
        router_row = router_ref[e]
        logit = jnp.sum(wide * router_row, axis=-1, keepdims=True)
        gate = 1.0 / (1.0 + jnp.exp(-logit))
        gate_low = gate.astype(jnp.bfloat16).astype(f32)
        total, gate_sum = 0.0, 0.0
        for c in range(chunks):
            for copy in copies[e, c]:
                copy.wait()
            weight, spread = ins[e, c], mul(cot_ref[e], outs[e, c], NT)
            activated, slope = gelu_parts(mul(slots, weight, NN))
            gate_sum += jnp.sum(activated * spread, axis=-1, keepdims=True)
            total += mul((gate_low * spread * slope).astype(jnp.bfloat16), weight, NT)
        grad_logit = gate_sum * gate * (1.0 - gate)
        grad_hidden = total + grad_logit * router_row
        back_ref[e] = grad_hidden.astype(jnp.bfloat16)
        small_ref[e, 0:1, :] = jnp.sum(wide * grad_logit, axis=0, keepdims=True)
        small_ref[e, 1:2, :] = jnp.sum(wide * grad_hidden, axis=0, keepdims=True) / gain_ref[...]


def experts(slot_hidden, slot_cot, expert_in, expert_out, router_rows, gain, earlier):
    count, slots, width = slot_hidden.shape
    hidden = expert_in.shape[2]
    chunk = min(hidden, 512)
    chunks = hidden // chunk
    return pl.pallas_call(
        functools.partial(expert_kernel, chunk),
        in_specs=[ANY] * (6 + len(earlier)),
        out_shape=[
            jax.ShapeDtypeStruct((count, slots, width), jnp.bfloat16),
            jax.ShapeDtypeStruct((count, 2, width), jnp.float32),
        ],
        scratch_shapes=[
            pltpu.VMEM((count, chunks, width, chunk), jnp.bfloat16),
            pltpu.VMEM((count, chunks, chunk, width), jnp.bfloat16),
            pltpu.SemaphoreType.DMA((2, count, chunks)),
            pltpu.VMEM(slot_hidden.shape, slot_hidden.dtype),
            pltpu.VMEM(slot_cot.shape, slot_cot.dtype),
            pltpu.VMEM(router_rows.shape, router_rows.dtype),
            pltpu.VMEM(gain.shape, gain.dtype),
            pltpu.SemaphoreType.DMA((4,)),
        ],
        compiler_params=params(),
        cost_estimate=pl.CostEstimate(
            flops=12 * count * slots * width * hidden, bytes_accessed=8 * count * slots * hidden, transcendentals=0
        ),
        name="experts",
    )(slot_hidden, slot_cot, router_rows, gain, expert_in, expert_out, *earlier)


def weights_kernel(units_ref, *refs):
    f32, bf16 = jnp.float32, jnp.bfloat16
    in_hbm, out_hbm = refs[5:7]
    far_in_ref, far_out_ref, up_ref, down_ref, own_ref, token_ref, ins, outs, sems = refs[-15:-6]
    hidden_refs, cot_refs, router_ref = refs[-6:-4], refs[-4:-2], refs[-2]
    few = bring(refs[:5], refs[-6:-1], refs[-1])
    count, ways, width, part = ins.shape
    copies = {}
    for e in range(count):
        for d in range(ways):
            units = pl.ds(pl.multiple_of(units_ref[d] * part, part), part)
            copies[e, d] = (
                pltpu.make_async_copy(in_hbm.at[e, :, units], ins.at[e, d], sems.at[0, e, d]),
                pltpu.make_async_copy(out_hbm.at[e, units, :], outs.at[e, d], sems.at[1, e, d]),
            )
            for copy in copies[e, d]:
                copy.start()
    token_ref[...] = jnp.zeros_like(token_ref)
    for copy in few:
        copy.wait()
    for e in range(count):
        slots = jnp.concatenate([r[e] for r in hidden_refs], axis=0)
        cot = jnp.concatenate([r[e] for r in cot_refs], axis=0)
        logit = jnp.sum(slots.astype(f32) * router_ref[e], axis=-1, keepdims=True)
        gate = (1.0 / (1.0 + jnp.exp(-logit))).astype(bf16).astype(f32)
        scaled = (gate * cot.astype(f32)).astype(bf16)
        slots_t, scaled_t = slots.T, scaled.T
        for d in range(ways):
            for copy in copies[e, d]:
                copy.wait()
            activated, slope = gelu_parts(mul(slots, ins[e, d], NN))
            grad_pre = (mul(scaled, outs[e, d], NT) * slope).astype(bf16)
            sum_in = mul(slots_t, grad_pre, NN)
            sum_out = mul(scaled_t, activated.astype(bf16), NN)
            if d == 0:
                far_in_ref[e] = sum_in.astype(bf16)
                far_out_ref[e] = sum_out.astype(bf16)
            else:
                target = (up_ref, down_ref, own_ref)[d - 1]
                target[0, e] = sum_in.astype(target.dtype)
                target[1, e] = sum_out.astype(target.dtype)


def weight_sums(hidden_rows, cot_rows, router_rows, expert_in, expert_out, earlier):
    count, slots, width = hidden_rows[0].shape
    along = lax.axis_size("x")
    part = expert_in.shape[2] // (2 * along)
    half, place = lax.axis_index("yh"), lax.axis_index("x")
    units = jnp.stack([half * along + (place + way) % along for way in (2, 1, -1, 0)]).astype(jnp.int32)
    bf16, f32 = jnp.bfloat16, jnp.float32
    return pl.pallas_call(
        weights_kernel,
        in_specs=[SMEM] + [ANY] * (7 + len(earlier)),
        out_shape=[jax.ShapeDtypeStruct((count, width, part), bf16)] * 2
        + [jax.ShapeDtypeStruct((2, count, width, part), t) for t in (bf16, bf16, f32)]
        + [jax.ShapeDtypeStruct((8, 128), f32)],
        scratch_shapes=[
            pltpu.VMEM((count, 4, width, part), bf16),
            pltpu.VMEM((count, 4, part, width), bf16),
            pltpu.SemaphoreType.DMA((2, count, 4)),
        ]
        + [pltpu.VMEM((count, slots, width), bf16)] * 4
        + [pltpu.VMEM(router_rows.shape, f32), pltpu.SemaphoreType.DMA((5,))],
        compiler_params=params(),
        cost_estimate=pl.CostEstimate(
            flops=128 * count * slots * width * part, bytes_accessed=16 * count * slots * width, transcendentals=0
        ),
        name="weight_sums",
    )(units, *hidden_rows, *cot_rows, router_rows, expert_in, expert_out, *earlier)


def join_kernel(up_ref, down_ref, far_in_ref, far_out_ref, *refs):
    up_out, down_out = refs[-2:]
    f32, bf16 = jnp.float32, jnp.bfloat16
    up_out[0] = (up_ref[0].astype(f32) + far_in_ref[...].astype(f32)).astype(bf16)
    up_out[1] = up_ref[1]
    down_out[0] = down_ref[0]
    down_out[1] = (down_ref[1].astype(f32) + far_out_ref[...].astype(f32)).astype(bf16)


def join(up, down, far_in, far_out, earlier):
    return on_staged(
        join_kernel,
        (up, down, far_in, far_out),
        earlier,
        [jax.ShapeDtypeStruct(up.shape, up.dtype)] * 2,
        "join",
    )


def weight_total_kernel(own_ref, up_ref, down_ref, grad_in_ref, grad_out_ref):
    f32 = jnp.float32
    total = own_ref[:, 0] + up_ref[:, 0].astype(f32) + down_ref[:, 0].astype(f32)
    grad_in_ref[0] = total[0].astype(jnp.bfloat16)
    grad_out_ref[0] = total[1].T.astype(jnp.bfloat16)


def weight_total(own, up, down):
    _, count, width, part = own.shape
    arrived = pl.BlockSpec((2, 1, width, part), lambda e: (0, e, 0, 0))
    return pl.pallas_call(
        weight_total_kernel,
        grid=(count,),
        in_specs=[arrived] * 3,
        out_specs=[
            pl.BlockSpec((1, width, part), lambda e: (e, 0, 0)),
            pl.BlockSpec((1, part, width), lambda e: (e, 0, 0)),
        ],
        out_shape=[
            jax.ShapeDtypeStruct((count, width, part), jnp.bfloat16),
            jax.ShapeDtypeStruct((count, part, width), jnp.bfloat16),
        ],
        compiler_params=params(),
        name="weight_total",
    )(own, up, down)


def quarter_of(tile_ref, q):
    half = tile_ref.shape[0] // 2
    a, b = q // 2, q % 2
    block = tile_ref[half * a : half * (a + 1), half * b : half * (b + 1), :]
    return block.reshape(half * half, tile_ref.shape[2])


def quarters_kernel(count, *refs):
    outs, (buffer, sems) = refs[count : count + 4], refs[-2:]
    copies = [pltpu.make_async_copy(refs[n], buffer.at[n], sems.at[n]) for n in range(count)]
    for copy in copies:
        copy.start()
    for n in range(count):
        copies[n].wait()
        for q in range(4):
            block = quarter_of(buffer.at[n], q)
            rows = block.shape[0]
            outs[q][rows * n : rows * (n + 1), :] = block


def quarters(tiles):
    side, _, width = tiles[0].shape
    count = len(tiles)
    return pl.pallas_call(
        functools.partial(quarters_kernel, count),
        in_specs=[ANY] * count,
        out_shape=[jax.ShapeDtypeStruct((count * side * side // 4, width), tiles[0].dtype)] * 4,
        scratch_shapes=[
            pltpu.VMEM((count, side, side, width), tiles[0].dtype),
            pltpu.SemaphoreType.DMA((count,)),
        ],
        compiler_params=params(),
        name="quarters",
    )(*tiles)


def tiles_kernel(count, *refs):
    for n in range(count):
        tile_ref = refs[4 + n]
        half, width = tile_ref.shape[0] // 2, tile_ref.shape[2]
        for q in range(4):
            a, b = q // 2, q % 2
            block = refs[q][half * half * n : half * half * (n + 1), :].reshape(half, half, width)
            tile_ref[half * a : half * (a + 1), half * b : half * (b + 1), :] = block


def tiles(parts, count, side):
    width = parts[0].shape[1]
    return pl.pallas_call(
        functools.partial(tiles_kernel, count),
        grid=(width // GROUP,),
        in_specs=[pl.BlockSpec((parts[0].shape[0], GROUP), lambda g: (0, g))] * 4,
        out_specs=[pl.BlockSpec((side, side, GROUP), lambda g: (0, 0, g))] * count,
        out_shape=[jax.ShapeDtypeStruct((side, side, width), parts[0].dtype)] * count,
        compiler_params=params(),
        name="tiles",
    )(*parts)


def slot_picker(place_ref, slots):
    place = place_ref[...]
    index = lax.broadcasted_iota(jnp.int32, (slots, place.shape[1]), 0)
    return (index == place).astype(jnp.bfloat16)


def to_slots_kernel(place_ref, cot_hbm, residual_hbm, *refs):
    slots_ref, cot_ref, residual_ref, buffer, sems = refs[-5:]
    copies = [
        pltpu.make_async_copy(hbm, buffer.at[n], sems.at[n]) for n, hbm in enumerate((cot_hbm, residual_hbm))
    ]
    for copy in copies:
        copy.start()
    for n, out in enumerate((cot_ref, residual_ref)):
        copies[n].wait()
        for q in range(4):
            block = quarter_of(buffer.at[n], q)
            rows = block.shape[0]
            out[rows * q : rows * (q + 1), :] = block
        if n == 0:
            picker = slot_picker(place_ref, slots_ref.shape[0])
            slots_ref[...] = mul(picker, cot_ref[...], NN).astype(slots_ref.dtype)


def to_slots(place, cotangent, residual, slots, earlier):
    side, _, width = cotangent.shape
    low = cotangent.dtype
    return pl.pallas_call(
        to_slots_kernel,
        in_specs=[VMEM, ANY, ANY] + [ANY] * len(earlier),
        out_shape=[jax.ShapeDtypeStruct((slots, width), low)]
        + [jax.ShapeDtypeStruct((side * side, width), low)] * 2,
        scratch_shapes=[pltpu.VMEM((2, side, side, width), low), pltpu.SemaphoreType.DMA((2,))],
        compiler_params=params(),
        name="to_slots",
    )(place, cotangent, residual, *earlier)


def norm_kernel(place_ref, gain_ref, proj_ref, *refs):
    f32, bf16 = jnp.float32, jnp.bfloat16
    mixed_refs = refs[:4]
    residual_ref, slots_ref, normed_ref, inv_ref = refs[4], *refs[-3:]
    mixed = jnp.concatenate([r[...] for r in mixed_refs], axis=0)
    attended = mul(mixed, proj_ref[...], NN).astype(bf16)
    stream = residual_ref[...].astype(f32) + attended.astype(f32)
    centered = stream - jnp.mean(stream, axis=-1, keepdims=True)
    inv_std = lax.rsqrt(jnp.mean(centered * centered, axis=-1, keepdims=True) + EPSILON)
    normed = centered * inv_std
    hidden_in = (normed * gain_ref[...]).astype(bf16)
    normed_ref[...] = normed
    inv_ref[...] = inv_std
    slots_ref[...] = mul(slot_picker(place_ref, slots_ref.shape[0]), hidden_in, NN).astype(bf16)


def norm(place, gain, out_proj, mixed, residual, slots, earlier):
    tokens, width = place.shape[1], out_proj.shape[0]
    return on_staged(
        norm_kernel,
        (place, gain, out_proj, *mixed, residual),
        earlier,
        [
            jax.ShapeDtypeStruct((slots, width), jnp.bfloat16),
            jax.ShapeDtypeStruct((tokens, width), jnp.float32),
            jax.ShapeDtypeStruct((tokens, 1), jnp.float32),
        ],
        "norm",
    )


def token_kernel(place_ref, gain_ref, proj_ref, returned_ref, normed_ref, inv_ref, *refs):
    f32, bf16 = jnp.float32, jnp.bfloat16
    mixed_refs, cot_ref = refs[:4], refs[4]
    grad_refs, grad_mixed_refs, part_ref = refs[-9:-5], refs[-5:-1], refs[-1]
    mixed = jnp.concatenate([r[...] for r in mixed_refs], axis=0)
    cot = cot_ref[...]
    normed, inv_std = normed_ref[...], inv_ref[...]
    grad_hidden = mul(slot_picker(place_ref, returned_ref.shape[0]), returned_ref[...], TN)
    grad = grad_hidden * gain_ref[...]
    grad_input = (
        cot.astype(f32)
        + inv_std
        * (
            grad
            - jnp.mean(grad, axis=-1, keepdims=True)
            - normed * jnp.mean(grad * normed, axis=-1, keepdims=True)
        )
    ).astype(bf16)
    grad_mixed = mul(grad_input, proj_ref[...], NT).astype(bf16)
    part_ref[...] = mul(mixed, grad_input, TN).astype(bf16)
    quarter = grad_refs[0].shape[0]
    for q in range(4):
        grad_refs[q][...] = grad_input[quarter * q : quarter * (q + 1), :]
        grad_mixed_refs[q][...] = grad_mixed[quarter * q : quarter * (q + 1), :]


def token_grads(place, gain, out_proj, returned, normed, inv_std, mixed, cot, earlier):
    tokens, width = normed.shape
    return on_staged(
        token_kernel,
        (place, gain, out_proj, returned, normed, inv_std, *mixed, cot),
        earlier,
        [jax.ShapeDtypeStruct((tokens // 4, width), jnp.bfloat16)] * 8
        + [jax.ShapeDtypeStruct((width, width), jnp.bfloat16)],
        "token_grads",
    )


def to_devices_kernel(rows_ref, *refs):
    out_ref = refs[-1]
    devices, rows, width = out_ref.shape
    count = rows_ref.shape[0]
    parts = [
        rows_ref[e].astype(jnp.float32).reshape(devices, rows // count, width) for e in range(count)
    ]
    out_ref[...] = jnp.concatenate(parts, axis=1).astype(out_ref.dtype)


def to_devices(rows, devices, earlier):
    count, slots, width = rows.shape
    shape = jax.ShapeDtypeStruct((devices, count * slots // devices, width), rows.dtype)
    return on_staged(to_devices_kernel, (rows,), earlier, shape, "to_devices")


def finish_kernel(part, count, summed_ref, *refs):
    proj_ref, gain_ref, further_ref = refs[-3:]
    devices, _, width = summed_ref.shape
    proj_ref[...] = summed_ref[:, :part, :].reshape(devices * part, width)
    further = summed_ref[:, part:, :].astype(jnp.float32)
    further_ref[...] = further
    gain_ref[...] = jnp.sum(further[:, count, :], axis=0, keepdims=True)


def finish(summed, part, count, earlier):
    devices, rows, width = summed.shape
    return on_staged(
        functools.partial(finish_kernel, part, count),
        (summed,),
        earlier,
        [
            jax.ShapeDtypeStruct((devices * part, width), summed.dtype),
            jax.ShapeDtypeStruct((1, width), jnp.float32),
            jax.ShapeDtypeStruct((devices, rows - part, width), jnp.float32),
        ],
        "finish",
    )


def share_kernel(further, shares_ref, *refs):
    total = jnp.sum(shares_ref[...].astype(jnp.float32), axis=0)
    out_ref = refs[-1]
    total = jnp.concatenate([total] + [r[...] for r in refs[:further]], axis=0).astype(jnp.bfloat16)
    out_ref[...] = jnp.broadcast_to(total[None], out_ref.shape)


def share_sum(inputs, copies, earlier):
    rows = inputs[0].shape[1] + sum(x.shape[0] for x in inputs[1:])
    shape = jax.ShapeDtypeStruct((copies, rows, inputs[0].shape[2]), inputs[0].dtype)
    kernel = functools.partial(share_kernel, len(inputs) - 1)
    return on_staged(kernel, inputs, earlier, shape, "share_sum")


def shards(
    queries,
    key_vectors,
    values,
    residual,
    cotangent,
    out_proj,
    norm_gain,
    router,
    expert_in,
    expert_out,
    expert_id,
    slot_index,
):
    f32, bf16 = jnp.float32, jnp.bfloat16
    side = queries.shape[0]
    width = queries.shape[2]
    head_size = width // HEADS
    tokens = side * side
    quarter = tokens // 4
    expert_count = router.shape[1]
    local_experts = expert_in.shape[0]
    capacity = 2 * tokens // expert_count
    slots_total = expert_count * capacity
    grid_rows, grid_cols = lax.axis_size(GY), lax.axis_size(GX)
    row, col = lax.axis_index(GY), lax.axis_index(GX)
    core = lax.axis_index("c")
    gain = norm_gain[None, :]

    pieces = image_to_window(quarters([queries, key_vectors, values]))

    place = (
        (expert_id * capacity + slot_index)
        .reshape(2, side // 2, 2, side // 2)
        .transpose(0, 2, 1, 3)
        .reshape(1, tokens)
    )
    cot_slots, cot, residual = to_slots(place, cotangent, residual, slots_total, pieces[1:])

    def exchange(slots):
        arrived = lax.all_to_all(slots, GX, 0, 0, tiled=True)
        return (
            arrived.reshape(grid_cols, local_experts, capacity, width)
            .transpose(1, 0, 2, 3)
            .reshape(local_experts, grid_cols * capacity, width)
        )

    slot_cot = exchange(cot_slots)
    other_cot = swap(slot_cot, "yh")

    last = (2 * (row == grid_rows - 1) + (col == grid_cols - 1)).astype(jnp.int32)[None]
    *mixed_win, probs = attend(last, pieces, quarter, head_size)
    mixed = window_to_image(mixed_win)

    slots, normed, inv_std = norm(place, gain, out_proj, mixed, residual, slots_total, ())

    slot_hidden = exchange(slots)
    other_hidden = swap(slot_hidden, "yh")
    router_rows = lax.dynamic_slice_in_dim(router, col * local_experts, local_experts, 1).T.astype(f32)[:, None]
    grad_hidden_slot, small = experts(
        slot_hidden, slot_cot, expert_in, expert_out, router_rows, gain, (other_cot,)
    )
    returning = to_devices(grad_hidden_slot, grid_cols, (other_hidden,))
    returned = lax.all_to_all(returning, GX, 0, 0, tiled=True).reshape(slots_total, width)

    far_in, far_out, upward, downward, own_sums, sums_done = weight_sums(
        (slot_hidden, other_hidden),
        (slot_cot, other_cot),
        router_rows,
        expert_in,
        expert_out,
        (small,),
    )
    far_in, far_out = step(far_in, 1), step(far_out, -1)
    outcome = token_grads(place, gain, out_proj, returned, normed, inv_std, mixed, cot, (sums_done,))
    grad_input, grad_mixed_image, proj_part = outcome[:4], outcome[4:8], outcome[8]
    grad_mixed = image_to_window(grad_mixed_image)
    upward, downward = join(upward, downward, far_in, far_out, grad_mixed[1:])
    from_below, from_above = step(upward, 1), step(downward, -1)

    grads = attend_back(pieces, grad_mixed, probs, quarter, head_size, ())

    extra = jnp.concatenate((small[:, 0], jnp.sum(small[:, 1], axis=0, keepdims=True)), axis=0)
    extra = jnp.pad(extra, ((0, -extra.shape[0] % 8), (0, 0)))
    shares = lax.all_to_all(proj_part.reshape(grid_cols, -1, width), GX, 0, 0, tiled=True)
    shares = lax.all_to_all(share_sum((shares, extra), grid_rows, (grads[0], upward)), GY, 0, 0, tiled=True)
    summed = lax.all_to_all(share_sum((shares,), grid_cols, (from_below, from_above)), GX, 0, 0, tiled=True)
    image_out = tiles(window_to_image(grads), 3, side)
    grad_proj, grad_gain, further = finish(summed, width // grid_cols, local_experts, image_out[:1])
    grad_router = further[:, :local_experts].reshape(expert_count, width).T
    grad_in, grad_out = weight_total(own_sums, from_below, from_above)

    return (
        image_out[0],
        image_out[1],
        image_out[2],
        tiles(grad_input, 1, side)[0],
        grad_proj,
        grad_gain[0],
        grad_router,
        grad_in,
        grad_out,
    )


def solution(mesh):
    rows, cols = mesh.devices.shape
    split = Mesh(mesh.devices.reshape(2, rows // 2, cols // 2, 2), EVERY)
    tile = P(GY, GX, None)
    return jax.shard_map(
        shards,
        mesh=split,
        in_specs=(tile,) * 5 + (P(), P(), P(), P(GX, None, None), P(GX, None, None), P(GY, GX), P(GY, GX)),
        out_specs=(tile,) * 4 + (P(), P(), P(), P(GX, None, GY), P(GX, GY, None)),
        check_vma=False,
    )
```

```python
import functools

import jax
import jax.numpy as jnp
from jax import lax
from jax.experimental import pallas as pl
from jax.experimental.pallas import tpu as pltpu
from jax.sharding import Mesh
from jax.sharding import PartitionSpec as P

HEADS = 16
EPSILON = 1e-05
NEGATIVE = -1e30
GELU_COEF = 0.7978845608028654
CUBIC_COEF = 0.044715
GY = ("yh", "x")
GX = ("g", "c")
EVERY = GY + GX
ANY = pl.BlockSpec(memory_space=pl.ANY)
VMEM = pl.BlockSpec(memory_space=pltpu.VMEM)
SMEM = pl.BlockSpec(memory_space=pltpu.SMEM)


def fetch(block, down, right):
    rows, cols = lax.axis_size(GY), lax.axis_size(GX)
    if down == 0 and right == 0:
        return block
    if down == 0:
        return lax.ppermute(block, GX, [((j + right) % cols, j) for j in range(cols)])
    if right == 0:
        return lax.ppermute(block, GY, [((i + down) % rows, i) for i in range(rows)])
    route = [
        (((i + down) % rows) * cols + (j + right) % cols, i * cols + j)
        for i in range(rows)
        for j in range(cols)
    ]
    return lax.ppermute(block, EVERY, route)


def swap(block, axis):
    return lax.ppermute(block, axis, [(0, 1), (1, 0)])


def step(block, way):
    size = lax.axis_size("x")
    return lax.ppermute(block, "x", [(i, (i + way) % size) for i in range(size)])


def image_to_window(quarters):
    return [fetch(quarters[3 - p], p // 2, p % 2) for p in range(4)]


def window_to_image(pieces):
    return [fetch(pieces[3 - q], -((3 - q) // 2), -((3 - q) % 2)) for q in range(4)]


def gelu_parts(inputs):
    square = inputs * inputs
    factor = GELU_COEF + (GELU_COEF * CUBIC_COEF) * square
    tangent = jnp.tanh(inputs * factor)
    share = 0.5 + 0.5 * tangent
    value = inputs * share
    slope = share + value * (1.0 - tangent) * (3.0 * factor - 2.0 * GELU_COEF)
    return value, slope

NN = (((1,), (0,)), ((), ()))
NT = (((1,), (1,)), ((), ()))
TN = (((0,), (0,)), ((), ()))
GROUP = 128


def mul(a, b, dims):
    return lax.dot_general(a, b, dims, preferred_element_type=jnp.float32)


def window_parts(pieces, quarter):
    return [
        jnp.concatenate([p[quarter * n : quarter * (n + 1), :] for p in pieces], axis=0) for n in range(3)
    ]


def attend_kernel(quarter, head_size, last_ref, *refs):
    pieces, mixed_refs, probs_ref = refs[:4], refs[-5:-1], refs[-1]
    query, key, value = window_parts(pieces, quarter)
    tokens = query.shape[0]
    of_key = lax.broadcasted_iota(jnp.int32, (tokens, tokens), 0)
    of_query = lax.broadcasted_iota(jnp.int32, (tokens, tokens), 1)
    differs = jnp.bitwise_xor(of_key // quarter, of_query // quarter)
    hidden = jnp.bitwise_and(differs, last_ref[0]) != 0
    scale = head_size ** (-0.5)
    lane_head = lax.broadcasted_iota(jnp.int32, query.shape, 1) // head_size
    value_t = value.T
    mixed_t = []
    for h in range(GROUP // head_size):
        masked = jnp.where(lane_head == h, query, jnp.zeros_like(query))
        scores = mul(key, masked, NT) * scale
        scores = jnp.where(hidden, NEGATIVE, scores)
        weights = jnp.exp(scores - jnp.max(scores, axis=0, keepdims=True))
        probs = (weights * (1.0 / jnp.sum(weights, axis=0, keepdims=True))).astype(jnp.bfloat16)
        probs_ref[h] = probs
        mixed_t.append(mul(value_t[h * head_size : (h + 1) * head_size, :], probs, NN))
    mixed = jnp.concatenate(mixed_t, axis=0).T.astype(jnp.bfloat16)
    for p in range(4):
        mixed_refs[p][...] = mixed[quarter * p : quarter * (p + 1), :]


def attend_back_kernel(quarter, head_size, *refs):
    pieces, grad_refs, probs_ref, outs = refs[:4], refs[4:8], refs[8], refs[-4:]
    query, key, value = window_parts(pieces, quarter)
    grad = jnp.concatenate([r[...] for r in grad_refs], axis=0)
    scale = head_size ** (-0.5)
    lane_head = lax.broadcasted_iota(jnp.int32, query.shape, 1) // head_size
    key_t = key.T
    grad_query_t = []
    grad_key = jnp.zeros(query.shape, jnp.float32)
    grad_value = jnp.zeros(query.shape, jnp.float32)
    for h in range(GROUP // head_size):
        mine = lane_head == h
        masked_grad = jnp.where(mine, grad, jnp.zeros_like(grad))
        masked_query = jnp.where(mine, query, jnp.zeros_like(query))
        probs_low = probs_ref[h]
        probs = probs_low.astype(jnp.float32)
        grad_probs = mul(value, masked_grad, NT)
        total = jnp.sum(probs * grad_probs, axis=0, keepdims=True)
        grad_scores = (probs * (grad_probs - total) * scale).astype(jnp.bfloat16)
        grad_value += mul(probs_low, masked_grad, NN)
        grad_key += mul(grad_scores, masked_query, NN)
        grad_query_t.append(mul(key_t[h * head_size : (h + 1) * head_size, :], grad_scores, NN))
    grad_query = jnp.concatenate(grad_query_t, axis=0).T
    for n, g in enumerate((grad_query, grad_key, grad_value)):
        low = g.astype(jnp.bfloat16)
        for p in range(4):
            outs[p][quarter * n : quarter * (n + 1), :] = low[quarter * p : quarter * (p + 1), :]


def staged(kernel, count, *refs):
    inputs, (buffers, sems) = refs[:count], (refs[-1 - count : -1], refs[-1])
    copies = [pltpu.make_async_copy(inputs[n], buffers[n], sems.at[n]) for n in range(count)]
    for copy in copies:
        copy.start()
    for copy in copies:
        copy.wait()
    kernel(*buffers, *refs[count : -1 - count])


def on_staged(kernel, inputs, earlier, out_shape, name, flops=0):
    return pl.pallas_call(
        functools.partial(staged, kernel, len(inputs)),
        in_specs=[ANY] * (len(inputs) + len(earlier)),
        out_shape=out_shape,
        scratch_shapes=[pltpu.VMEM(x.shape, x.dtype) for x in inputs]
        + [pltpu.SemaphoreType.DMA((len(inputs),))],
        compiler_params=params(),
        cost_estimate=pl.CostEstimate(flops=flops, bytes_accessed=1, transcendentals=0),
        name=name,
    )(*inputs, *earlier)


def params():
    return pltpu.CompilerParams(vmem_limit_bytes=60 * 1024 * 1024)


def attend(last, pieces, quarter, head_size):
    tokens, width = 4 * quarter, pieces[0].shape[1]
    heads, groups = GROUP // head_size, width // GROUP
    return pl.pallas_call(
        functools.partial(attend_kernel, quarter, head_size),
        grid=(groups,),
        in_specs=[SMEM]
        + [pl.BlockSpec((3 * quarter, GROUP), lambda g: (0, g))] * 4,
        out_specs=[pl.BlockSpec((quarter, GROUP), lambda g: (0, g))] * 4
        + [pl.BlockSpec((heads, tokens, tokens), lambda g: (g, 0, 0))],
        out_shape=[jax.ShapeDtypeStruct((quarter, width), jnp.bfloat16)] * 4
        + [jax.ShapeDtypeStruct((width // head_size, tokens, tokens), jnp.bfloat16)],
        compiler_params=params(),
        cost_estimate=pl.CostEstimate(
            flops=16 * tokens * tokens * width, bytes_accessed=12 * tokens * width, transcendentals=0
        ),
        name="attend",
    )(last, *pieces)


def attend_back(pieces, grads, probs, quarter, head_size, earlier):
    tokens, width = 4 * quarter, pieces[0].shape[1]
    heads, groups = GROUP // head_size, width // GROUP
    return pl.pallas_call(
        functools.partial(attend_back_kernel, quarter, head_size),
        grid=(groups,),
        in_specs=[pl.BlockSpec((3 * quarter, GROUP), lambda g: (0, g))] * 4
        + [pl.BlockSpec((quarter, GROUP), lambda g: (0, g))] * 4
        + [pl.BlockSpec((heads, tokens, tokens), lambda g: (g, 0, 0))]
        + [ANY] * len(earlier),
        out_specs=[pl.BlockSpec((3 * quarter, GROUP), lambda g: (0, g))] * 4,
        out_shape=[jax.ShapeDtypeStruct((3 * quarter, width), jnp.bfloat16)] * 4,
        compiler_params=params(),
        cost_estimate=pl.CostEstimate(
            flops=8 * tokens * tokens * width * 4, bytes_accessed=12 * tokens * width * 2, transcendentals=0
        ),
        name="attend_back",
    )(*pieces, *grads, probs, *earlier)


def bring(sources, buffers, sems):
    copies = [pltpu.make_async_copy(s, b, sems.at[n]) for n, (s, b) in enumerate(zip(sources, buffers))]
    for copy in copies:
        copy.start()
    return copies


def expert_kernel(chunk, hidden_hbm, cot_hbm, router_hbm, gain_hbm, in_hbm, out_hbm, *refs):
    back_ref, small_ref, ins, outs, sems, hidden_ref, cot_ref, router_ref, gain_ref, few_sems = refs[-10:]
    f32 = jnp.float32
    count, chunks = ins.shape[:2]
    few = bring(
        (hidden_hbm, router_hbm, cot_hbm, gain_hbm), (hidden_ref, router_ref, cot_ref, gain_ref), few_sems
    )
    copies = {}
    for e in range(count):
        for c in range(chunks):
            units = pl.ds(chunk * c, chunk)
            copies[e, c] = (
                pltpu.make_async_copy(in_hbm.at[e, :, units], ins.at[e, c], sems.at[0, e, c]),
                pltpu.make_async_copy(out_hbm.at[e, units, :], outs.at[e, c], sems.at[1, e, c]),
            )
            for copy in copies[e, c]:
                copy.start()
    for copy in few:
        copy.wait()
    for e in range(count):
        slots = hidden_ref[e]
        wide = slots.astype(f32)
        router_row = router_ref[e]
        logit = jnp.sum(wide * router_row, axis=-1, keepdims=True)
        gate = 1.0 / (1.0 + jnp.exp(-logit))
        gate_low = gate.astype(jnp.bfloat16).astype(f32)
        total, gate_sum = 0.0, 0.0
        for c in range(chunks):
            for copy in copies[e, c]:
                copy.wait()
            weight, spread = ins[e, c], mul(cot_ref[e], outs[e, c], NT)
            activated, slope = gelu_parts(mul(slots, weight, NN))
            gate_sum += jnp.sum(activated * spread, axis=-1, keepdims=True)
            total += mul((gate_low * spread * slope).astype(jnp.bfloat16), weight, NT)
        grad_logit = gate_sum * gate * (1.0 - gate)
        grad_hidden = total + grad_logit * router_row
        back_ref[e] = grad_hidden.astype(jnp.bfloat16)
        small_ref[e, 0:1, :] = jnp.sum(wide * grad_logit, axis=0, keepdims=True)
        small_ref[e, 1:2, :] = jnp.sum(wide * grad_hidden, axis=0, keepdims=True) / gain_ref[...]


def experts(slot_hidden, slot_cot, expert_in, expert_out, router_rows, gain, earlier):
    count, slots, width = slot_hidden.shape
    hidden = expert_in.shape[2]
    chunk = min(hidden, 512)
    chunks = hidden // chunk
    return pl.pallas_call(
        functools.partial(expert_kernel, chunk),
        in_specs=[ANY] * (6 + len(earlier)),
        out_shape=[
            jax.ShapeDtypeStruct((count, slots, width), jnp.bfloat16),
            jax.ShapeDtypeStruct((count, 2, width), jnp.float32),
        ],
        scratch_shapes=[
            pltpu.VMEM((count, chunks, width, chunk), jnp.bfloat16),
            pltpu.VMEM((count, chunks, chunk, width), jnp.bfloat16),
            pltpu.SemaphoreType.DMA((2, count, chunks)),
            pltpu.VMEM(slot_hidden.shape, slot_hidden.dtype),
            pltpu.VMEM(slot_cot.shape, slot_cot.dtype),
            pltpu.VMEM(router_rows.shape, router_rows.dtype),
            pltpu.VMEM(gain.shape, gain.dtype),
            pltpu.SemaphoreType.DMA((4,)),
        ],
        compiler_params=params(),
        cost_estimate=pl.CostEstimate(
            flops=12 * count * slots * width * hidden, bytes_accessed=8 * count * slots * hidden, transcendentals=0
        ),
        name="experts",
    )(slot_hidden, slot_cot, router_rows, gain, expert_in, expert_out, *earlier)


def weights_kernel(units_ref, *refs):
    f32, bf16 = jnp.float32, jnp.bfloat16
    in_hbm, out_hbm = refs[5:7]
    far_in_ref, far_out_ref, up_ref, down_ref, own_ref, token_ref, ins, outs, sems = refs[-15:-6]
    hidden_refs, cot_refs, router_ref = refs[-6:-4], refs[-4:-2], refs[-2]
    few = bring(refs[:5], refs[-6:-1], refs[-1])
    count, ways, width, part = ins.shape
    copies = {}
    for e in range(count):
        for d in range(ways):
            units = pl.ds(pl.multiple_of(units_ref[d] * part, part), part)
            copies[e, d] = (
                pltpu.make_async_copy(in_hbm.at[e, :, units], ins.at[e, d], sems.at[0, e, d]),
                pltpu.make_async_copy(out_hbm.at[e, units, :], outs.at[e, d], sems.at[1, e, d]),
            )
            for copy in copies[e, d]:
                copy.start()
    token_ref[...] = jnp.zeros_like(token_ref)
    for copy in few:
        copy.wait()
    for e in range(count):
        slots = jnp.concatenate([r[e] for r in hidden_refs], axis=0)
        cot = jnp.concatenate([r[e] for r in cot_refs], axis=0)
        logit = jnp.sum(slots.astype(f32) * router_ref[e], axis=-1, keepdims=True)
        gate = (1.0 / (1.0 + jnp.exp(-logit))).astype(bf16).astype(f32)
        scaled = (gate * cot.astype(f32)).astype(bf16)
        slots_t, scaled_t = slots.T, scaled.T
        for d in range(ways):
            for copy in copies[e, d]:
                copy.wait()
            activated, slope = gelu_parts(mul(slots, ins[e, d], NN))
            grad_pre = (mul(scaled, outs[e, d], NT) * slope).astype(bf16)
            sum_in = mul(slots_t, grad_pre, NN)
            sum_out = mul(scaled_t, activated.astype(bf16), NN)
            if d == 0:
                far_in_ref[e] = sum_in.astype(bf16)
                far_out_ref[e] = sum_out.astype(bf16)
            else:
                target = (up_ref, down_ref, own_ref)[d - 1]
                target[0, e] = sum_in.astype(target.dtype)
                target[1, e] = sum_out.astype(target.dtype)


def weight_sums(hidden_rows, cot_rows, router_rows, expert_in, expert_out, earlier):
    count, slots, width = hidden_rows[0].shape
    along = lax.axis_size("x")
    part = expert_in.shape[2] // (2 * along)
    half, place = lax.axis_index("yh"), lax.axis_index("x")
    units = jnp.stack([half * along + (place + way) % along for way in (2, 1, -1, 0)]).astype(jnp.int32)
    bf16, f32 = jnp.bfloat16, jnp.float32
    return pl.pallas_call(
        weights_kernel,
        in_specs=[SMEM] + [ANY] * (7 + len(earlier)),
        out_shape=[jax.ShapeDtypeStruct((count, width, part), bf16)] * 2
        + [jax.ShapeDtypeStruct((2, count, width, part), t) for t in (bf16, bf16, f32)]
        + [jax.ShapeDtypeStruct((8, 128), f32)],
        scratch_shapes=[
            pltpu.VMEM((count, 4, width, part), bf16),
            pltpu.VMEM((count, 4, part, width), bf16),
            pltpu.SemaphoreType.DMA((2, count, 4)),
        ]
        + [pltpu.VMEM((count, slots, width), bf16)] * 4
        + [pltpu.VMEM(router_rows.shape, f32), pltpu.SemaphoreType.DMA((5,))],
        compiler_params=params(),
        cost_estimate=pl.CostEstimate(
            flops=128 * count * slots * width * part, bytes_accessed=16 * count * slots * width, transcendentals=0
        ),
        name="weight_sums",
    )(units, *hidden_rows, *cot_rows, router_rows, expert_in, expert_out, *earlier)


def join_kernel(up_ref, down_ref, far_in_ref, far_out_ref, *refs):
    up_out, down_out = refs[-2:]
    f32, bf16 = jnp.float32, jnp.bfloat16
    up_out[0] = (up_ref[0].astype(f32) + far_in_ref[...].astype(f32)).astype(bf16)
    up_out[1] = up_ref[1]
    down_out[0] = down_ref[0]
    down_out[1] = (down_ref[1].astype(f32) + far_out_ref[...].astype(f32)).astype(bf16)


def join(up, down, far_in, far_out, earlier):
    return on_staged(
        join_kernel,
        (up, down, far_in, far_out),
        earlier,
        [jax.ShapeDtypeStruct(up.shape, up.dtype)] * 2,
        "join",
    )


def weight_total_kernel(own_ref, up_ref, down_ref, grad_in_ref, grad_out_ref):
    f32 = jnp.float32
    total = own_ref[:, 0] + up_ref[:, 0].astype(f32) + down_ref[:, 0].astype(f32)
    grad_in_ref[0] = total[0].astype(jnp.bfloat16)
    grad_out_ref[0] = total[1].T.astype(jnp.bfloat16)


def weight_total(own, up, down):
    _, count, width, part = own.shape
    arrived = pl.BlockSpec((2, 1, width, part), lambda e: (0, e, 0, 0))
    return pl.pallas_call(
        weight_total_kernel,
        grid=(count,),
        in_specs=[arrived] * 3,
        out_specs=[
            pl.BlockSpec((1, width, part), lambda e: (e, 0, 0)),
            pl.BlockSpec((1, part, width), lambda e: (e, 0, 0)),
        ],
        out_shape=[
            jax.ShapeDtypeStruct((count, width, part), jnp.bfloat16),
            jax.ShapeDtypeStruct((count, part, width), jnp.bfloat16),
        ],
        compiler_params=params(),
        name="weight_total",
    )(own, up, down)


def quarter_of(tile_ref, q):
    half = tile_ref.shape[0] // 2
    a, b = q // 2, q % 2
    block = tile_ref[half * a : half * (a + 1), half * b : half * (b + 1), :]
    return block.reshape(half * half, tile_ref.shape[2])


def quarters_kernel(count, *refs):
    outs, (buffer, sems) = refs[count : count + 4], refs[-2:]
    copies = [pltpu.make_async_copy(refs[n], buffer.at[n], sems.at[n]) for n in range(count)]
    for copy in copies:
        copy.start()
    for n in range(count):
        copies[n].wait()
        for q in range(4):
            block = quarter_of(buffer.at[n], q)
            rows = block.shape[0]
            outs[q][rows * n : rows * (n + 1), :] = block


def quarters(tiles):
    side, _, width = tiles[0].shape
    count = len(tiles)
    return pl.pallas_call(
        functools.partial(quarters_kernel, count),
        in_specs=[ANY] * count,
        out_shape=[jax.ShapeDtypeStruct((count * side * side // 4, width), tiles[0].dtype)] * 4,
        scratch_shapes=[
            pltpu.VMEM((count, side, side, width), tiles[0].dtype),
            pltpu.SemaphoreType.DMA((count,)),
        ],
        compiler_params=params(),
        name="quarters",
    )(*tiles)


def tiles_kernel(count, *refs):
    for n in range(count):
        tile_ref = refs[4 + n]
        half, width = tile_ref.shape[0] // 2, tile_ref.shape[2]
        for q in range(4):
            a, b = q // 2, q % 2
            block = refs[q][half * half * n : half * half * (n + 1), :].reshape(half, half, width)
            tile_ref[half * a : half * (a + 1), half * b : half * (b + 1), :] = block


def tiles(parts, count, side):
    width = parts[0].shape[1]
    return pl.pallas_call(
        functools.partial(tiles_kernel, count),
        grid=(width // GROUP,),
        in_specs=[pl.BlockSpec((parts[0].shape[0], GROUP), lambda g: (0, g))] * 4,
        out_specs=[pl.BlockSpec((side, side, GROUP), lambda g: (0, 0, g))] * count,
        out_shape=[jax.ShapeDtypeStruct((side, side, width), parts[0].dtype)] * count,
        compiler_params=params(),
        name="tiles",
    )(*parts)


def slot_picker(place_ref, slots):
    place = place_ref[...]
    index = lax.broadcasted_iota(jnp.int32, (slots, place.shape[1]), 0)
    return (index == place).astype(jnp.bfloat16)


def to_slots_kernel(place_ref, cot_hbm, residual_hbm, *refs):
    slots_ref, cot_ref, residual_ref, buffer, sems = refs[-5:]
    copies = [
        pltpu.make_async_copy(hbm, buffer.at[n], sems.at[n]) for n, hbm in enumerate((cot_hbm, residual_hbm))
    ]
    for copy in copies:
        copy.start()
    for n, out in enumerate((cot_ref, residual_ref)):
        copies[n].wait()
        for q in range(4):
            block = quarter_of(buffer.at[n], q)
            rows = block.shape[0]
            out[rows * q : rows * (q + 1), :] = block
        if n == 0:
            picker = slot_picker(place_ref, slots_ref.shape[0])
            slots_ref[...] = mul(picker, cot_ref[...], NN).astype(slots_ref.dtype)


def to_slots(place, cotangent, residual, slots, earlier):
    side, _, width = cotangent.shape
    low = cotangent.dtype
    return pl.pallas_call(
        to_slots_kernel,
        in_specs=[VMEM, ANY, ANY] + [ANY] * len(earlier),
        out_shape=[jax.ShapeDtypeStruct((slots, width), low)]
        + [jax.ShapeDtypeStruct((side * side, width), low)] * 2,
        scratch_shapes=[pltpu.VMEM((2, side, side, width), low), pltpu.SemaphoreType.DMA((2,))],
        compiler_params=params(),
        name="to_slots",
    )(place, cotangent, residual, *earlier)


def norm_kernel(place_ref, gain_ref, proj_ref, *refs):
    f32, bf16 = jnp.float32, jnp.bfloat16
    mixed_refs = refs[:4]
    residual_ref, slots_ref, normed_ref, inv_ref = refs[4], *refs[-3:]
    mixed = jnp.concatenate([r[...] for r in mixed_refs], axis=0)
    attended = mul(mixed, proj_ref[...], NN).astype(bf16)
    stream = residual_ref[...].astype(f32) + attended.astype(f32)
    centered = stream - jnp.mean(stream, axis=-1, keepdims=True)
    inv_std = lax.rsqrt(jnp.mean(centered * centered, axis=-1, keepdims=True) + EPSILON)
    normed = centered * inv_std
    hidden_in = (normed * gain_ref[...]).astype(bf16)
    normed_ref[...] = normed
    inv_ref[...] = inv_std
    slots_ref[...] = mul(slot_picker(place_ref, slots_ref.shape[0]), hidden_in, NN).astype(bf16)


def norm(place, gain, out_proj, mixed, residual, slots, earlier):
    tokens, width = place.shape[1], out_proj.shape[0]
    return on_staged(
        norm_kernel,
        (place, gain, out_proj, *mixed, residual),
        earlier,
        [
            jax.ShapeDtypeStruct((slots, width), jnp.bfloat16),
            jax.ShapeDtypeStruct((tokens, width), jnp.float32),
            jax.ShapeDtypeStruct((tokens, 1), jnp.float32),
        ],
        "norm",
    )


def token_kernel(place_ref, gain_ref, proj_ref, returned_ref, normed_ref, inv_ref, *refs):
    f32, bf16 = jnp.float32, jnp.bfloat16
    mixed_refs, cot_ref = refs[:4], refs[4]
    grad_refs, grad_mixed_refs, part_ref = refs[-9:-5], refs[-5:-1], refs[-1]
    mixed = jnp.concatenate([r[...] for r in mixed_refs], axis=0)
    cot = cot_ref[...]
    normed, inv_std = normed_ref[...], inv_ref[...]
    grad_hidden = mul(slot_picker(place_ref, returned_ref.shape[0]), returned_ref[...], TN)
    grad = grad_hidden * gain_ref[...]
    grad_input = (
        cot.astype(f32)
        + inv_std
        * (
            grad
            - jnp.mean(grad, axis=-1, keepdims=True)
            - normed * jnp.mean(grad * normed, axis=-1, keepdims=True)
        )
    ).astype(bf16)
    grad_mixed = mul(grad_input, proj_ref[...], NT).astype(bf16)
    part_ref[...] = mul(mixed, grad_input, TN).astype(bf16)
    quarter = grad_refs[0].shape[0]
    for q in range(4):
        grad_refs[q][...] = grad_input[quarter * q : quarter * (q + 1), :]
        grad_mixed_refs[q][...] = grad_mixed[quarter * q : quarter * (q + 1), :]


def token_grads(place, gain, out_proj, returned, normed, inv_std, mixed, cot, earlier):
    tokens, width = normed.shape
    return on_staged(
        token_kernel,
        (place, gain, out_proj, returned, normed, inv_std, *mixed, cot),
        earlier,
        [jax.ShapeDtypeStruct((tokens // 4, width), jnp.bfloat16)] * 8
        + [jax.ShapeDtypeStruct((width, width), jnp.bfloat16)],
        "token_grads",
    )


def to_devices_kernel(rows_ref, *refs):
    out_ref = refs[-1]
    devices, rows, width = out_ref.shape
    count = rows_ref.shape[0]
    parts = [
        rows_ref[e].astype(jnp.float32).reshape(devices, rows // count, width) for e in range(count)
    ]
    out_ref[...] = jnp.concatenate(parts, axis=1).astype(out_ref.dtype)


def to_devices(rows, devices, earlier):
    count, slots, width = rows.shape
    shape = jax.ShapeDtypeStruct((devices, count * slots // devices, width), rows.dtype)
    return on_staged(to_devices_kernel, (rows,), earlier, shape, "to_devices")


def finish_kernel(part, count, summed_ref, *refs):
    proj_ref, gain_ref, further_ref = refs[-3:]
    devices, _, width = summed_ref.shape
    proj_ref[...] = summed_ref[:, :part, :].reshape(devices * part, width)
    further = summed_ref[:, part:, :].astype(jnp.float32)
    further_ref[...] = further
    gain_ref[...] = jnp.sum(further[:, count, :], axis=0, keepdims=True)


def finish(summed, part, count, earlier):
    devices, rows, width = summed.shape
    return on_staged(
        functools.partial(finish_kernel, part, count),
        (summed,),
        earlier,
        [
            jax.ShapeDtypeStruct((devices * part, width), summed.dtype),
            jax.ShapeDtypeStruct((1, width), jnp.float32),
            jax.ShapeDtypeStruct((devices, rows - part, width), jnp.float32),
        ],
        "finish",
    )


def share_kernel(further, shares_ref, *refs):
    total = jnp.sum(shares_ref[...].astype(jnp.float32), axis=0)
    out_ref = refs[-1]
    total = jnp.concatenate([total] + [r[...] for r in refs[:further]], axis=0).astype(jnp.bfloat16)
    out_ref[...] = jnp.broadcast_to(total[None], out_ref.shape)


def share_sum(inputs, copies, earlier):
    rows = inputs[0].shape[1] + sum(x.shape[0] for x in inputs[1:])
    shape = jax.ShapeDtypeStruct((copies, rows, inputs[0].shape[2]), inputs[0].dtype)
    kernel = functools.partial(share_kernel, len(inputs) - 1)
    return on_staged(kernel, inputs, earlier, shape, "share_sum")


def shards(
    queries,
    key_vectors,
    values,
    residual,
    cotangent,
    out_proj,
    norm_gain,
    router,
    expert_in,
    expert_out,
    expert_id,
    slot_index,
):
    f32, bf16 = jnp.float32, jnp.bfloat16
    side = queries.shape[0]
    width = queries.shape[2]
    head_size = width // HEADS
    tokens = side * side
    quarter = tokens // 4
    expert_count = router.shape[1]
    local_experts = expert_in.shape[0]
    capacity = 2 * tokens // expert_count
    slots_total = expert_count * capacity
    grid_rows, grid_cols = lax.axis_size(GY), lax.axis_size(GX)
    row, col = lax.axis_index(GY), lax.axis_index(GX)
    core = lax.axis_index("c")
    gain = norm_gain[None, :]

    pieces = image_to_window(quarters([queries, key_vectors, values]))

    place = (
        (expert_id * capacity + slot_index)
        .reshape(2, side // 2, 2, side // 2)
        .transpose(0, 2, 1, 3)
        .reshape(1, tokens)
    )
    cot_slots, cot, residual = to_slots(place, cotangent, residual, slots_total, pieces[1:])

    def exchange(slots):
        arrived = lax.all_to_all(slots, GX, 0, 0, tiled=True)
        return (
            arrived.reshape(grid_cols, local_experts, capacity, width)
            .transpose(1, 0, 2, 3)
            .reshape(local_experts, grid_cols * capacity, width)
        )

    slot_cot = exchange(cot_slots)
    other_cot = swap(slot_cot, "yh")

    last = (2 * (row == grid_rows - 1) + (col == grid_cols - 1)).astype(jnp.int32)[None]
    *mixed_win, probs = attend(last, pieces, quarter, head_size)
    mixed = window_to_image(mixed_win)

    slots, normed, inv_std = norm(place, gain, out_proj, mixed, residual, slots_total, ())

    slot_hidden = exchange(slots)
    other_hidden = swap(slot_hidden, "yh")
    router_rows = lax.dynamic_slice_in_dim(router, col * local_experts, local_experts, 1).T.astype(f32)[:, None]
    grad_hidden_slot, small = experts(
        slot_hidden, slot_cot, expert_in, expert_out, router_rows, gain, (other_cot,)
    )
    returning = to_devices(grad_hidden_slot, grid_cols, (other_hidden,))
    returned = lax.all_to_all(returning, GX, 0, 0, tiled=True).reshape(slots_total, width)

    far_in, far_out, upward, downward, own_sums, sums_done = weight_sums(
        (slot_hidden, other_hidden),
        (slot_cot, other_cot),
        router_rows,
        expert_in,
        expert_out,
        (small,),
    )
    far_in, far_out = step(far_in, 1), step(far_out, -1)
    outcome = token_grads(place, gain, out_proj, returned, normed, inv_std, mixed, cot, (sums_done,))
    grad_input, grad_mixed_image, proj_part = outcome[:4], outcome[4:8], outcome[8]
    grad_mixed = image_to_window(grad_mixed_image)
    upward, downward = join(upward, downward, far_in, far_out, grad_mixed[1:])
    from_below, from_above = step(upward, 1), step(downward, -1)

    grads = attend_back(pieces, grad_mixed, probs, quarter, head_size, ())

    image_out = tiles(window_to_image(grads), 3, side)

    extra = jnp.concatenate((small[:, 0], jnp.sum(small[:, 1], axis=0, keepdims=True)), axis=0)
    extra = jnp.pad(extra, ((0, -extra.shape[0] % 8), (0, 0)))
    shares = lax.all_to_all(proj_part.reshape(grid_cols, -1, width), GX, 0, 0, tiled=True)
    shares = lax.all_to_all(share_sum((shares, extra), grid_rows, (grads[0], upward)), GY, 0, 0, tiled=True)
    summed = lax.all_to_all(share_sum((shares,), grid_cols, (from_below, from_above, image_out[0])), GX, 0, 0, tiled=True)
    grad_proj, grad_gain, further = finish(summed, width // grid_cols, local_experts, image_out[:1])
    grad_router = further[:, :local_experts].reshape(expert_count, width).T
    grad_in, grad_out = weight_total(own_sums, from_below, from_above)

    return (
        image_out[0],
        image_out[1],
        image_out[2],
        tiles(grad_input, 1, side)[0],
        grad_proj,
        grad_gain[0],
        grad_router,
        grad_in,
        grad_out,
    )


def solution(mesh):
    rows, cols = mesh.devices.shape
    split = Mesh(mesh.devices.reshape(2, rows // 2, cols // 2, 2), EVERY)
    tile = P(GY, GX, None)
    return jax.shard_map(
        shards,
        mesh=split,
        in_specs=(tile,) * 5 + (P(), P(), P(), P(GX, None, None), P(GX, None, None), P(GY, GX), P(GY, GX)),
        out_specs=(tile,) * 4 + (P(), P(), P(), P(GX, None, GY), P(GX, GY, None)),
        check_vma=False,
    )
```
